256 devices in a mesh: inst: 4 (over x), surf: 32 (over z, y_lo, core), half: 2 (over y_hi).
Axes of the slice: x: 4, y: 4 (y_hi: 2, y_lo: 2; y = y_hi * 2 + y_lo), z: 8, core: 2. Of those that a mesh axis runs over, the one named last changes fastest.
Arguments:
- nodes: float32 [3, 262144], P(None, ('surf', 'half')), may hold values from 0 to 0.5
- surf_coords: float32 [8, 3, 32768], P('inst', None, 'surf'), may hold values from 0 to 0.5
- surf_weights: float32 [8, 3, 32768], P('inst', None, 'surf'), may hold values from -0.3 to 0.3
- tile_node: int32 [32, 2, 32, 24], P('surf', 'half'), may hold values from 0 to 31
- tile_surf: int32 [32, 2, 32, 24], P('surf', 'half'), may hold values from 0 to 7
- tile_count: int32 [32, 2, 32], P('surf', 'half'), may hold values from 0 to 24, as said below
- bnd_index: int32 [64, 2, 64], P(('surf', 'half')), may hold values from 0 to 4095
- bnd_count: int32 [64, 2], P(('surf', 'half')), may hold values from 1 to 64, as said below
Outputs:
- deformed: float32 [8, 3, 262144], P('inst', None, ('surf', 'half'))
- ghosts: float32 [8, 3, 8192], P('inst', None, ('surf', 'half'))
The draws below stay inside these ranges and needn't reach their ends.
Inputs may be any that keep to these rules, and one draw needn't show every extreme that they name: `tile_count`: every node block owner has, for some surface shard, exactly 24 live tiles. `bnd_count`: some owner's side has exactly 64 live boundary nodes.
All inputs are finite; a program needn't handle non-finite values.
Results may differ from the reference program's by a relative error of at most 0.00017.
Values sent between devices are 32-bit elements; how exact they have to be, the bound alone decides.
A program may use at most 64 MiB of HBM per device.

```python
import jax
import jax.numpy as jnp
from jax import lax

NODES_PER_DEVICE = 4096
SURF_DEV = 1024
TMAX = 24
BMAX = 64
INSTANCES = 8
NODES = 262144
SURF_PTS = 32768
BLOCKS = 64
N_SURF = 32
N_HALF = 2


def draw_tile_count(key, part):
    key = jax.random.fold_in(key, 11)
    first, second = jax.random.split(key)
    counts = jax.random.randint(first, (N_SURF, N_HALF, N_SURF), 0, TMAX + 1)
    where_full = jax.random.randint(second, (N_SURF, N_HALF, 1), 0, N_SURF)
    shards = jnp.arange(N_SURF, dtype=jnp.int32)[None, None, :]
    return jnp.where(shards == where_full, TMAX, counts).astype(jnp.int32)


def draw_bnd_count(key, part):
    key = jax.random.fold_in(key, 23)
    first, second = jax.random.split(key)
    counts = jax.random.randint(first, (N_SURF * N_HALF, 2), 1, BMAX + 1)
    where_full = jax.random.randint(second, (), 0, N_SURF * N_HALF * 2)
    flat = jnp.arange(N_SURF * N_HALF * 2, dtype=jnp.int32).reshape(N_SURF * N_HALF, 2)
    return jnp.where(flat == where_full, BMAX, counts).astype(jnp.int32)


def plant(array, rng, low, high):
    longest = array.shape.index(max(array.shape))
    spots = []
    for shift in (0, 1):
        where = [jax.random.randint(jax.random.fold_in(rng, axis), (), 0, length) for axis, length in enumerate(array.shape)]
        where[longest] = (where[longest] + shift) % array.shape[longest]
        spots.append(tuple(where))
    return array.at[spots[0]].set(low).at[spots[1]].set(high)


def block_levels(stream_key, dims, cuts, low, largest):
    level = 1.0
    for axis_at, blocks in cuts:
        steps = jax.random.uniform(jax.random.fold_in(jax.random.fold_in(stream_key, 6), axis_at), (blocks,), jnp.float32, low / len(cuts), largest / len(cuts))
        level = level * jnp.repeat(jnp.exp(steps), dims[axis_at] // blocks).reshape((-1,) + (1,) * (len(dims) - 1 - axis_at))
    return level


def scatter_about(key, extent, spread, limit, cuts=(), kind=jnp.bfloat16):
    drawn = spread * jax.random.normal(key, extent, jnp.float32)
    if cuts:
        drawn = drawn * block_levels(key, extent, cuts, -0.22, 0.18)
    return jnp.clip(drawn, -limit, limit).astype(kind)


def setup_inputs(seed: int = 0) -> dict:
    key_of = jax.random.split(jax.random.key(seed), 9)
    return {
        "nodes": jnp.clip(0.5 * jax.random.uniform(key_of[0], (3, NODES), jnp.float32) ** block_levels(key_of[0], (3, NODES), ((1, 64),), -0.2, 0.2), 0.0, 0.5),
        "surf_coords": jnp.clip(0.5 * jax.random.uniform(key_of[1], (INSTANCES, 3, SURF_PTS), jnp.float32) ** block_levels(key_of[1], (INSTANCES, 3, SURF_PTS), ((0, 4), (2, 32)), -0.2, 0.2), 0.0, 0.5),
        "surf_weights": scatter_about(key_of[2], (INSTANCES, 3, SURF_PTS), 0.05, 0.3, ((0, 4), (2, 32)), jnp.float32),
        "tile_node": plant(jax.random.randint(key_of[3], (N_SURF, N_HALF, N_SURF, TMAX), 0, NODES_PER_DEVICE // 128), jax.random.fold_in(key_of[3], 1), 0, (NODES_PER_DEVICE // 128) - 1).astype(jnp.int32),
        "tile_surf": plant(jax.random.randint(key_of[4], (N_SURF, N_HALF, N_SURF, TMAX), 0, SURF_DEV // 128), jax.random.fold_in(key_of[4], 1), 0, (SURF_DEV // 128) - 1).astype(jnp.int32),
        "tile_count": draw_tile_count(jax.random.fold_in(key_of[8], 71), 0),
        "bnd_index": plant(jax.random.randint(key_of[6], (BLOCKS, 2, BMAX), 0, NODES_PER_DEVICE), jax.random.fold_in(key_of[6], 1), 0, NODES_PER_DEVICE - 1).astype(jnp.int32),
        "bnd_count": draw_bnd_count(jax.random.fold_in(key_of[8], 71), 0),
    }


RADIUS = 0.4
HARMONIC = 0.8

def tile_terms(node_portion, coord_part, weight_part):
    delta = node_portion[None, :, :, :, None] - coord_part[:, :, :, None, :]
    dist = jnp.sqrt(lax.optimization_barrier(jnp.sum(delta * delta, axis=1))) / RADIUS
    inner = jnp.maximum(1.0 - dist, 0.0)
    phi = inner ** 4 * (4.0 * dist + 1.0)
    return jnp.einsum('ignm,icgm->icgn', phi, weight_part, precision=lax.Precision.HIGHEST)

def reference(nodes, surf_coords, surf_weights, tile_node, tile_surf, tile_count, bnd_index, bnd_count):
    node_blocks = NODES_PER_DEVICE // 128
    surface_blocks = SURF_DEV // 128
    count_inst = surf_coords.shape[0]
    node_window = nodes.reshape(3, NODES // 128, 128)
    coord_view = surf_coords.reshape(count_inst, 3, SURF_PTS // 128, 128)
    weight_view = surf_weights.reshape(count_inst, 3, SURF_PTS // 128, 128)
    disp = jnp.zeros((count_inst, 3, NODES // 128, 128), jnp.float32)
    slot_numbers = jnp.arange(TMAX, dtype=jnp.int32)

    def per_pair(flat, acc):
        owner = (flat // N_SURF).astype(jnp.int32)
        shard = (flat % N_SURF).astype(jnp.int32)
        srow = owner // N_HALF
        hrow = owner % N_HALF
        node_idx = (owner * node_blocks + tile_node[srow, hrow, shard]).astype(jnp.int32)
        surf_idx = (shard * surface_blocks + tile_surf[srow, hrow, shard]).astype(jnp.int32)
        live = slot_numbers < tile_count[srow, hrow, shard]
        node_portion = jnp.take(node_window, node_idx, axis=1)
        coord_part = jnp.take(coord_view, surf_idx, axis=2)
        weight_part = jnp.take(weight_view, surf_idx, axis=2)
        term = jnp.where(live[None, None, :, None], tile_terms(node_portion, coord_part, weight_part), 0.0)
        return acc.at[:, :, node_idx, :].add(term)
    disp = lax.fori_loop(0, BLOCKS * N_SURF, per_pair, disp)
    disp = disp.reshape(count_inst, 3, NODES)
    spectral = lax.optimization_barrier(jnp.sum(disp, axis=0)) / count_inst
    deformed = nodes[None] + spectral[None] + HARMONIC * (disp - spectral[None])
    per_block = deformed.reshape(count_inst, 3, BLOCKS, NODES_PER_DEVICE)
    slots = jnp.arange(BMAX)

    def send_list(block, side):
        picked = jnp.take(per_block[:, :, block, :], bnd_index[block, side], axis=2)
        return jnp.where(slots[None, None, :] < bnd_count[block, side], picked, 0.0)
    pieces = []
    for block in range(BLOCKS):
        srow = block // N_HALF
        if srow > 0:
            lower = send_list(block - N_HALF, 1)
        else:
            lower = jnp.zeros((count_inst, 3, BMAX), jnp.float32)
        if srow < N_SURF - 1:
            upper = send_list(block + N_HALF, 0)
        else:
            upper = jnp.zeros((count_inst, 3, BMAX), jnp.float32)
        pieces.append(lower)
        pieces.append(upper)
    ghosts = jnp.concatenate(pieces, axis=2)
    return (deformed, ghosts)
```

```python
import functools

import jax
import jax.numpy as jnp
from jax import lax
from jax.experimental import pallas as pl
from jax.experimental.pallas import tpu as pltpu
from jax.sharding import PartitionSpec as P

RADIUS = 0.4
HARMONIC = 0.8
CENTRE = 0.25
UNROLL = 24

f32 = jnp.float32
bf16 = jnp.bfloat16
MESH = pl.DeviceIdType.MESH
NN = (((1,), (0,)), ((), ()))
TN = (((0,), (0,)), ((), ()))


def split3(x):
    a = x.astype(bf16)
    rest = x - a.astype(f32)
    b = rest.astype(bf16)
    c = (rest - b.astype(f32)).astype(bf16)
    return a, b, c


def rows_of(shape):
    return lax.broadcasted_iota(jnp.int32, shape, 0)


def stack_two(ref):
    n = ref.shape[2]
    gap = jnp.zeros((1, n), f32)
    return jnp.concatenate([ref[0], gap, ref[1], gap], axis=0)


def node_tables(nodes_ref, n_ref):
    row = rows_of((8, 128))
    blocks = nodes_ref.shape[1] // 128

    def one(b, _):
        x = (nodes_ref[:, pl.ds(pl.multiple_of(b * 128, 128), 128)] - CENTRE) * (1.0 / RADIUS)
        sq = x * x
        p = sq[0:1] + sq[1:2] + sq[2:3]
        four = jnp.concatenate([-2.0 * x, jnp.ones((1, 128), f32)], axis=0)
        eight = jnp.concatenate([four, four], axis=0)
        left, right = jnp.where(row < 4, eight, 0.0), jnp.where(row < 4, 0.0, eight)
        wide = jnp.concatenate([left, right], axis=1)
        b0, b1, b2 = split3(wide)
        p0, p1, p2 = split3(jnp.concatenate([p, p], axis=1))
        zero = jnp.zeros((13, 256), f32)
        tail = jnp.concatenate([p0.astype(f32), p1.astype(f32), p2.astype(f32), zero], axis=0).astype(bf16)
        n_ref[b, 0:16] = jnp.concatenate([b0, b0], axis=0)
        n_ref[b, 16:32] = jnp.concatenate([b1, b1], axis=0)
        n_ref[b, 32:48] = jnp.concatenate([b2, b0], axis=0)
        n_ref[b, 48:64] = tail
        return 0

    lax.fori_loop(0, blocks, one, 0)


def surface_tables(held, j, s_ref, w_ref):
    c = (held[j, 0:8] - CENTRE) * (1.0 / RADIUS)
    w = held[j, 8:16] * 4.0
    row = rows_of(c.shape)
    sq = c * c
    q = pltpu.roll(sq, 1, 0) + pltpu.roll(sq, 2, 0) + pltpu.roll(sq, 3, 0)
    a0, a1, a2 = split3(jnp.where(row % 4 == 3, q, c))
    first = jnp.concatenate([a0, a1], axis=0)
    second = jnp.concatenate([a0, a2], axis=0)
    hi = w.astype(bf16)
    both = jnp.concatenate([hi, (w - hi.astype(f32)).astype(bf16)], axis=0)
    per = c.shape[1] // 128
    for b in range(per):
        at = slice(b * 128, b * 128 + 128)
        s_ref[j * per + b, 0:16] = first[:, at]
        s_ref[j * per + b, 16:32] = second[:, at]
        w_ref[j * per + b] = both[:, at]


def gather_kernel(nodes_ref, coords_ref, weights_ref, n_ref, s_ref, w_ref,
                  held, zs, zr, bs, br, ys, yr, os_, or_, cs, cr):
    surf, half = lax.axis_index("surf"), lax.axis_index("half")
    z, y_lo, core = surf // 4, (surf // 2) % 2, surf % 2
    ring = 8
    inst = lax.axis_index("inst")

    def at(zz, yy, cc):
        return (zz % ring) * 4 + yy * 2 + cc

    up = (inst, at(z + 1, y_lo, core), half)
    down = (inst, at(z + ring - 1, y_lo, core), half)
    beside = (inst, at(z, 1 - y_lo, core), half)
    across = (inst, at(z, 1 - y_lo, core), 1 - half)
    twin = (inst, at(z, y_lo, 1 - core), half)

    barrier = pltpu.get_barrier_semaphore()
    for other in (up, down, beside, across, twin):
        pl.semaphore_signal(barrier, inc=1, device_id=other, device_id_type=MESH)
    pl.semaphore_wait(barrier, 5)

    def copy(ref, send, recv, to):
        return pltpu.make_async_remote_copy(
            src_ref=ref, dst_ref=ref, send_sem=send, recv_sem=recv, device_id=to, device_id_type=MESH
        )

    def zcopy(k, sign, yy, cc, block):
        if sign > 0:
            return copy(held.at[block], zs.at[k - 1], zr.at[k - 1], up)
        return copy(held.at[block], bs.at[k - 1], br.at[k - 1], down)

    def ycopies(q, block):
        return (
            copy(held.at[block, pl.ds(0, 8)], ys.at[q], yr.at[q], beside),
            copy(held.at[block, pl.ds(8, 8)], os_.at[q], or_.at[q], across),
        )

    def ccopy(q, block):
        return copy(held.at[block], cs.at[q], cr.at[q], twin)

    mine = at(z, y_lo, core)
    held[mine, 0:8] = stack_two(coords_ref)
    held[mine, 8:16] = stack_two(weights_ref)
    sent = []

    def go(c):
        c.start()
        sent.append(c)

    offsets = [0, -1, 1, -2, 2, -3, 3, -4]

    def own(q):
        return at(z + ring + offsets[q], y_lo, core)

    def other(q):
        return at(z + ring + offsets[q], 1 - y_lo, core)

    def spread(q):
        for c in ycopies(q, own(q)):
            go(c)
        go(ccopy(q, own(q)))

    go(zcopy(1, 1, y_lo, core, mine))
    go(zcopy(1, -1, y_lo, core, mine))
    spread(0)
    last = s_ref.shape[0] - 1
    s_ref[last] = jnp.zeros_like(s_ref[last])
    w_ref[last] = jnp.zeros_like(w_ref[last])
    surface_tables(held, mine, s_ref, w_ref)
    node_tables(nodes_ref, n_ref)

    def take_other(q):
        for c in ycopies(q, other(q)):
            c.wait_recv()
        go(ccopy(8 + q, other(q)))
        surface_tables(held, other(q), s_ref, w_ref)

    for q in range(1, 8):
        k = abs(offsets[q])
        sign = 1 if offsets[q] < 0 else -1
        zcopy(k, sign, y_lo, core, own(q)).wait_recv()
        if k < (4 if sign > 0 else 3):
            go(zcopy(k + 1, sign, y_lo, core, own(q)))
        spread(q)
        surface_tables(held, own(q), s_ref, w_ref)
        take_other(q - 1)
    take_other(7)
    for q in range(16):
        block = at(z + ring + offsets[q % 8], y_lo if q < 8 else 1 - y_lo, 1 - core)
        ccopy(q, block).wait_recv()
        surface_tables(held, block, s_ref, w_ref)
    for c in sent:
        c.wait_send()


def gather(nodes, coords, weights):
    n_surf = lax.axis_size("surf")
    points = coords.shape[2]
    blocks = n_surf * points // 128
    vmem = pl.BlockSpec(memory_space=pltpu.VMEM)
    dma = pltpu.SemaphoreType.DMA
    return pl.pallas_call(
        gather_kernel,
        out_shape=(
            jax.ShapeDtypeStruct((nodes.shape[1] // 128, 64, 256), bf16),
            jax.ShapeDtypeStruct((blocks + 1, 32, 128), bf16),
            jax.ShapeDtypeStruct((blocks + 1, 16, 128), bf16),
        ),
        in_specs=[vmem] * 3,
        out_specs=(vmem,) * 3,
        scratch_shapes=[
            pltpu.VMEM((n_surf, 16, points), f32),
            dma((4,)), dma((4,)), dma((3,)), dma((3,)),
            dma((8,)), dma((8,)), dma((8,)), dma((8,)),
            dma((16,)), dma((16,)),
        ],
        compiler_params=pltpu.CompilerParams(
            collective_id=0, has_side_effects=True, vmem_limit_bytes=32 * 1024 * 1024
        ),
        name="gather",
    )(nodes, coords, weights)


def tile_sum(s, n, w):
    ones = jnp.ones((16, 128), bf16)
    left = jnp.concatenate([s[0:16], s[0:16], s[16:32], ones], axis=0)
    dist2 = lax.dot_general(left, n, TN, preferred_element_type=f32)
    dist = pl.reciprocal(lax.rsqrt(lax.clamp(0.0, dist2, 1.0)), approx=True)
    inner = 1.0 - dist
    inner2 = inner * inner
    phi = (inner2 * inner2) * (0.25 + dist)
    hi = phi.astype(bf16)
    lo = (phi - hi.astype(f32)).astype(bf16)
    return lax.dot_general(
        jnp.concatenate([w, w], axis=1), jnp.concatenate([hi, lo], axis=0), NN,
        preferred_element_type=f32,
    )


def tiles_kernel(node_list, surf_list, counts, n_ref, s_ref, w_ref, disp_ref, acc, codes):
    shards, most = node_list.shape[2], node_list.shape[3]
    per = (s_ref.shape[0] - 1) // shards
    dummy = s_ref.shape[0] - 1

    def flatten(o, pos):
        for t in range(most):
            codes[pos + t] = node_list[0, 0, o, t] * 512 + (surf_list[0, 0, o, t] + o * per)
        return pos + counts[0, 0, o]

    total = lax.fori_loop(0, shards, flatten, 0)
    for t in range(UNROLL):
        codes[total + t] = dummy
    acc[...] = jnp.zeros_like(acc)

    def group(g, _):
        found = []
        for u in range(UNROLL):
            code = codes[g * UNROLL + u]
            node, surf = code // 512, code % 512
            found.append((node, tile_sum(s_ref[surf], n_ref[node], w_ref[surf])))
        for node, term in found:
            acc[node] += term
        return 0

    lax.fori_loop(0, (total + UNROLL - 1) // UNROLL, group, 0)
    row = rows_of((8, 128))
    for b in range(acc.shape[0]):
        one = acc[b, 0:8] + acc[b, 8:16]
        disp_ref[:, b * 128:b * 128 + 128] = jnp.where(row < 4, one[:, 0:128], one[:, 128:256])


def tiles(tile_node, tile_surf, tile_count, n_table, s_table, w_table):
    vmem = pl.BlockSpec(memory_space=pltpu.VMEM)
    smem = pl.BlockSpec(memory_space=pltpu.SMEM)
    node_blocks = n_table.shape[0]
    slots = tile_node.shape[2] * tile_node.shape[3]
    return pl.pallas_call(
        tiles_kernel,
        out_shape=jax.ShapeDtypeStruct((8, node_blocks * 128), f32),
        in_specs=[smem] * 3 + [vmem] * 3,
        out_specs=vmem,
        scratch_shapes=[
            pltpu.VMEM((node_blocks, 16, 256), f32),
            pltpu.SMEM((slots + 2 * UNROLL,), jnp.int32),
        ],
        compiler_params=pltpu.CompilerParams(vmem_limit_bytes=32 * 1024 * 1024),
        name="tiles",
    )(tile_node, tile_surf, tile_count, n_table, s_table, w_table)


def finish_kernel(disp_ref, nodes_ref, index_ref, count_ref, out_ref, ghost_ref,
                  part, outlist, inlist, xs, xr, gs, gr):
    inst, surf, half = lax.axis_index("inst"), lax.axis_index("surf"), lax.axis_index("half")
    n_inst, n_surf = 4, lax.axis_size("surf")
    after = (inst, (surf + 1) % n_surf, half)
    before = (inst, (surf + n_surf - 1) % n_surf, half)
    peers = [((inst + d) % n_inst, surf, half) for d in range(1, n_inst)]
    barrier = pltpu.get_barrier_semaphore()
    for to in peers + [after, before]:
        pl.semaphore_signal(barrier, inc=1, device_id=to, device_id_type=MESH)

    wide = disp_ref.shape[1]
    mid = wide // 2
    disp = disp_ref[...]
    both = disp + pltpu.roll(disp, 4, 0)
    part[0] = jnp.where(rows_of((8, mid)) < 4, both[:, :mid], both[:, mid:])
    pl.semaphore_wait(barrier, n_inst + 1)
    copies = [
        pltpu.make_async_remote_copy(
            src_ref=part.at[0], dst_ref=part.at[d], send_sem=xs.at[d - 1], recv_sem=xr.at[d - 1],
            device_id=peers[d - 1], device_id_type=MESH,
        )
        for d in range(1, n_inst)
    ]
    for c in copies:
        c.start()

    index = jnp.concatenate([index_ref[0, 0:1, :], index_ref[0, 1:2, :]], axis=1)
    slots = index.shape[1] // 2
    lane = lax.broadcasted_iota(jnp.int32, (8, 2 * slots), 1)
    live = lane < jnp.where(lane < slots, count_ref[0, 0], count_ref[0, 1] + slots)
    pick = (rows_of((128, 2 * slots)) == index % 128).astype(f32).astype(bf16)
    block = index // 128
    gap = jnp.zeros((1, wide), f32)
    nodes = nodes_ref[...]
    nodes8 = jnp.concatenate([nodes, gap, nodes, gap], axis=0)

    for c in copies:
        c.wait_recv()
    total = (part[0] + part[1] + part[2] + part[3]) * (1.0 / (2 * n_inst))
    swapped = pltpu.roll(total, 4, 0)
    low = rows_of((8, mid)) < 4
    spectral = jnp.concatenate([jnp.where(low, total, swapped), jnp.where(low, swapped, total)], axis=1)
    deformed = nodes8 + spectral + HARMONIC * (disp - spectral)
    out_ref[0] = deformed[0:3]
    out_ref[1] = deformed[4:7]

    tall = jnp.concatenate([deformed[:, b * 128:b * 128 + 128] for b in range(wide // 128)], axis=0)
    picked = sum(lax.dot_general(piece, pick, NN, preferred_element_type=f32) for piece in split3(tall))
    chosen = jnp.zeros((8, 2 * slots), f32)
    for b in range(wide // 128):
        chosen += jnp.where(block == b, picked[b * 8:b * 8 + 8], 0.0)
    chosen = jnp.where(live, chosen, 0.0)
    outlist[...] = chosen
    lists = [
        pltpu.make_async_remote_copy(
            src_ref=outlist, dst_ref=inlist.at[e], send_sem=gs.at[e], recv_sem=gr.at[e],
            device_id=to, device_id_type=MESH,
        )
        for e, to in enumerate((before, after))
    ]
    for c in lists:
        c.start()
    for c in lists:
        c.wait_recv()
    lower = jnp.where(surf > 0, inlist[1], 0.0)
    upper = jnp.where(surf < n_surf - 1, inlist[0], 0.0)
    shown = jnp.concatenate([lower[:, slots:], upper[:, :slots]], axis=1)
    ghost_ref[0] = shown[0:3]
    ghost_ref[1] = shown[4:7]
    for c in copies + lists:
        c.wait_send()


def finish(disp, nodes, bnd_index, bnd_count):
    vmem = pl.BlockSpec(memory_space=pltpu.VMEM)
    smem = pl.BlockSpec(memory_space=pltpu.SMEM)
    dma = pltpu.SemaphoreType.DMA
    wide, slots = nodes.shape[1], bnd_index.shape[2]
    return pl.pallas_call(
        finish_kernel,
        out_shape=(
            jax.ShapeDtypeStruct((2, 3, wide), f32),
            jax.ShapeDtypeStruct((2, 3, 2 * slots), f32),
        ),
        in_specs=[vmem, vmem, vmem, smem],
        out_specs=(vmem, vmem),
        scratch_shapes=[
            pltpu.VMEM((4, 8, wide // 2), f32),
            pltpu.VMEM((8, 2 * slots), f32),
            pltpu.VMEM((2, 8, 2 * slots), f32),
            dma((3,)), dma((3,)), dma((2,)), dma((2,)),
        ],
        compiler_params=pltpu.CompilerParams(
            collective_id=1, has_side_effects=True, vmem_limit_bytes=32 * 1024 * 1024
        ),
        name="finish",
    )(disp, nodes, bnd_index, bnd_count)


def shards(nodes, surf_coords, surf_weights, tile_node, tile_surf, tile_count, bnd_index, bnd_count):
    n_table, s_table, w_table = gather(nodes, surf_coords, surf_weights)
    disp = tiles(tile_node, tile_surf, tile_count, n_table, s_table, w_table)
    return finish(disp, nodes, bnd_index, bnd_count)


def solution(mesh):
    in_specs = (
        P(None, ("surf", "half")),
        P("inst", None, "surf"),
        P("inst", None, "surf"),
        P("surf", "half", None, None),
        P("surf", "half", None, None),
        P("surf", "half", None),
        P(("surf", "half"), None, None),
        P(("surf", "half"), None),
    )
    out_specs = (P("inst", None, ("surf", "half")), P("inst", None, ("surf", "half")))
    return jax.shard_map(shards, mesh=mesh, in_specs=in_specs, out_specs=out_specs, check_vma=False)
```

```python
import functools

import jax
import jax.numpy as jnp
from jax import lax
from jax.experimental import pallas as pl
from jax.experimental.pallas import tpu as pltpu
from jax.sharding import PartitionSpec as P

RADIUS = 0.4
HARMONIC = 0.8
CENTRE = 0.25
UNROLL = 24

f32 = jnp.float32
bf16 = jnp.bfloat16
MESH = pl.DeviceIdType.MESH
NN = (((1,), (0,)), ((), ()))
TN = (((0,), (0,)), ((), ()))


def split3(x):
    a = x.astype(bf16)
    rest = x - a.astype(f32)
    b = rest.astype(bf16)
    c = (rest - b.astype(f32)).astype(bf16)
    return a, b, c


def rows_of(shape):
    return lax.broadcasted_iota(jnp.int32, shape, 0)


def node_tables(nodes_ref, n_ref):
    row = rows_of((8, 128))
    blocks = nodes_ref.shape[1] // 128

    def one(b, _):
        x = (nodes_ref[:, pl.ds(pl.multiple_of(b * 128, 128), 128)] - CENTRE) * (1.0 / RADIUS)
        sq = x * x
        p = sq[0:1] + sq[1:2] + sq[2:3]
        four = jnp.concatenate([-2.0 * x, jnp.ones((1, 128), f32)], axis=0)
        eight = jnp.concatenate([four, four], axis=0)
        left, right = jnp.where(row < 4, eight, 0.0), jnp.where(row < 4, 0.0, eight)
        wide = jnp.concatenate([left, right], axis=1)
        b0, b1, b2 = split3(wide)
        p0, p1, p2 = split3(jnp.concatenate([p, p], axis=1))
        zero = jnp.zeros((13, 256), f32)
        tail = jnp.concatenate([p0.astype(f32), p1.astype(f32), p2.astype(f32), zero], axis=0).astype(bf16)
        n_ref[b, 0:16] = jnp.concatenate([b0, b0], axis=0)
        n_ref[b, 16:32] = jnp.concatenate([b1, b1], axis=0)
        n_ref[b, 32:48] = jnp.concatenate([b2, b0], axis=0)
        n_ref[b, 48:64] = tail
        return 0

    lax.fori_loop(0, blocks, one, 0)


def surface_tables(held, j, s_ref, w_ref):
    raw = jnp.concatenate([held[j, 0], held[j, 1]], axis=0)
    rest = held[j, 2]
    row = rows_of(raw.shape)
    c = (raw - CENTRE) * (1.0 / RADIUS)
    sq = c * c
    q = pltpu.roll(sq, 1, 0) + pltpu.roll(sq, 2, 0) + pltpu.roll(sq, 3, 0)
    a0, a1, a2 = split3(jnp.where(row % 4 == 3, q, c))
    first = jnp.concatenate([a0, a1], axis=0)
    second = jnp.concatenate([a0, a2], axis=0)
    w = jnp.concatenate([rest, rest[3:4], rest[0:3]], axis=0)
    w = jnp.where(row % 4 == 3, raw, w) * 4.0
    hi = w.astype(bf16)
    both = jnp.concatenate([hi, (w - hi.astype(f32)).astype(bf16)], axis=0)
    per = c.shape[1] // 128
    for b in range(per):
        at = slice(b * 128, b * 128 + 128)
        s_ref[j * per + b, 0:16] = first[:, at]
        s_ref[j * per + b, 16:32] = second[:, at]
        w_ref[j * per + b] = both[:, at]


def compact(node_list, surf_list, counts, codes_ref, per, dummy):
    most, n = node_list.shape
    size = codes_ref.shape[1]
    lane = lax.broadcasted_iota(jnp.int32, (most, n), 1)
    code = node_list[...] * 512 + surf_list[...] + lane * per
    count = counts[...]
    wide = jnp.broadcast_to(count.astype(f32), (8, n)).astype(bf16)
    earlier = (rows_of((n, n)) < lax.broadcasted_iota(jnp.int32, (n, n), 1)).astype(f32).astype(bf16)
    base = lax.dot_general(wide, earlier, NN, preferred_element_type=f32)[0:1].astype(jnp.int32)
    slot = rows_of((most, n))
    dest = jnp.where(slot < count, base + slot, -1)
    place = lax.broadcasted_iota(jnp.int32, (most, size), 1)
    found = jnp.zeros((most, size), jnp.int32)
    for o in range(n):
        found += jnp.where(dest[:, o:o + 1] == place, code[:, o:o + 1], 0)
    total = (base + count)[:, n - 1:n]
    line = lax.broadcasted_iota(jnp.int32, (1, size), 1)
    listed = jnp.sum(found, axis=0, keepdims=True) + jnp.where(line >= total, dummy, 0)
    codes_ref[...] = jnp.where(line == size - 1, total, listed)


def gather_kernel(nodes_hbm, coords_hbm, weights_hbm, node_list_hbm, surf_list_hbm, counts_hbm,
                  n_ref, s_ref, w_ref, codes_ref,
                  held, nodes_in, coords_in, weights_in, node_list, surf_list, counts, local,
                  zs, zr, ys, yr, cs, cr):
    inst, surf, half = lax.axis_index("inst"), lax.axis_index("surf"), lax.axis_index("half")
    z, y_lo, core = surf // 4, (surf // 2) % 2, surf % 2
    ring = 8

    def at(zz, yy, cc):
        return (zz % ring) * 4 + yy * 2 + cc

    def along(d):
        return (inst, at(z + ring + d, y_lo, core), half)

    beside = (inst, at(z, 1 - y_lo, core), half)
    across = (inst, at(z, 1 - y_lo, core), 1 - half)
    twin = (inst, at(z, y_lo, 1 - core), half)

    barrier = pltpu.get_barrier_semaphore()
    for other in (along(1), along(-1), along(2), along(-2), beside, across, twin):
        pl.semaphore_signal(barrier, inc=1, device_id=other, device_id_type=MESH)
    pairs = (
        (coords_hbm, coords_in), (weights_hbm, weights_in), (nodes_hbm, nodes_in),
        (node_list_hbm.at[0, 0], node_list), (surf_list_hbm.at[0, 0], surf_list), (counts_hbm.at[0], counts),
    )
    loads = [pltpu.make_async_copy(src, dst, local.at[i]) for i, (src, dst) in enumerate(pairs)]
    for c in loads:
        c.start()
    per = coords_in.shape[2] // 128
    last = s_ref.shape[0] - 1
    s_ref[last] = jnp.zeros_like(s_ref[last])
    w_ref[last] = jnp.zeros_like(w_ref[last])
    mine = at(z, y_lo, core)
    loads[0].wait()
    loads[1].wait()
    c_in, w_in = coords_in, weights_in
    for i in range(2):
        held[mine, i] = jnp.concatenate([c_in[k, i:i + 1] for k in range(3)] + [w_in[0, i:i + 1]], axis=0)
    held[mine, 2] = jnp.concatenate([w_in[k, i:i + 1] for i in range(2) for k in (1, 2)], axis=0)

    mid = coords_in.shape[2] // 2
    low, high = pl.ds(0, mid), pl.ds(mid, mid)
    offsets = [0, -1, 1, -2, 2, -3, 3, 4]

    def copy(ref, send, recv, to):
        return pltpu.make_async_remote_copy(
            src_ref=ref, dst_ref=ref, send_sem=send, recv_sem=recv, device_id=to, device_id_type=MESH
        )

    def part(block, lanes=None):
        return held.at[block] if lanes is None else held.at[block, :, :, lanes]

    def own(d):
        return at(z + ring + d, y_lo, core)

    def other(d):
        return at(z + ring + d, 1 - y_lo, core)

    routes = {
        1: (1, 0, None), 2: (-1, 0, None), 3: (2, 0, None), 4: (-2, 0, None),
        5: (1, -2, None), 6: (-1, 2, None), 7: (2, -2, low), 0: (-2, 2, high),
    }

    def zcopy(r, arriving=False):
        step, origin, lanes = routes[r]
        block = own(origin - step) if arriving else own(origin)
        return copy(part(block, lanes), zs.at[r], zr.at[r], along(step))

    def ycopies(q, block):
        return (
            copy(part(block, low), ys.at[q], yr.at[q], beside),
            copy(part(block, high), ys.at[8 + q], yr.at[8 + q], across),
        )

    def ccopy(q, block):
        return copy(part(block), cs.at[q], cr.at[q], twin)

    sent = []

    def go(c):
        c.start()
        sent.append(c)

    def spread(q):
        for c in ycopies(q, own(offsets[q])):
            go(c)
        go(ccopy(q, own(offsets[q])))
        surface_tables(held, own(offsets[q]), s_ref, w_ref)

    def take_other(q):
        for c in ycopies(q, other(offsets[q])):
            c.wait_recv()
        go(ccopy(8 + q, other(offsets[q])))
        surface_tables(held, other(offsets[q]), s_ref, w_ref)

    pl.semaphore_wait(barrier, 7)
    for r in (1, 2, 3, 4):
        go(zcopy(r))
    spread(0)
    for c in loads[2:]:
        c.wait()
    node_tables(nodes_in, n_ref)
    compact(node_list, surf_list, counts, codes_ref, per, last)

    zcopy(1, True).wait_recv()
    spread(1)
    zcopy(2, True).wait_recv()
    spread(2)
    take_other(0)
    zcopy(3, True).wait_recv()
    go(zcopy(5))
    go(zcopy(7))
    spread(3)
    zcopy(4, True).wait_recv()
    go(zcopy(6))
    go(zcopy(0))
    spread(4)
    for q in (1, 2, 3, 4):
        take_other(q)
    zcopy(5, True).wait_recv()
    spread(5)
    zcopy(6, True).wait_recv()
    spread(6)
    zcopy(7, True).wait_recv()
    zcopy(0, True).wait_recv()
    spread(7)
    for q in (5, 6, 7):
        take_other(q)
    for q in range(16):
        block = at(z + ring + offsets[q % 8], y_lo if q < 8 else 1 - y_lo, 1 - core)
        ccopy(q, block).wait_recv()
        surface_tables(held, block, s_ref, w_ref)
    for c in sent:
        c.wait_send()


def gather(nodes, coords, weights, tile_node, tile_surf, tile_count):
    arrays = (nodes, coords, weights, tile_node, tile_surf, tile_count)
    n_surf = lax.axis_size("surf")
    points = coords.shape[2]
    blocks = n_surf * points // 128
    most, n = tile_node.shape[2:]
    size = most * n + 128
    vmem = pl.BlockSpec(memory_space=pltpu.VMEM)
    dma = pltpu.SemaphoreType.DMA
    return pl.pallas_call(
        gather_kernel,
        out_shape=(
            jax.ShapeDtypeStruct((nodes.shape[1] // 128, 64, 256), bf16),
            jax.ShapeDtypeStruct((blocks + 1, 32, 128), bf16),
            jax.ShapeDtypeStruct((blocks + 1, 16, 128), bf16),
            jax.ShapeDtypeStruct((1, size), jnp.int32),
        ),
        in_specs=[pl.BlockSpec(memory_space=pltpu.HBM)] * 6,
        out_specs=(vmem,) * 4,
        scratch_shapes=[
            pltpu.VMEM((n_surf, 3, 4, points), f32),
            pltpu.VMEM(nodes.shape, f32),
            pltpu.VMEM(coords.shape, f32),
            pltpu.VMEM(weights.shape, f32),
            pltpu.VMEM((most, n), jnp.int32),
            pltpu.VMEM((most, n), jnp.int32),
            pltpu.VMEM((1, n), jnp.int32),
            dma((6,)),
            dma((8,)), dma((8,)), dma((16,)), dma((16,)), dma((16,)), dma((16,)),
        ],
        compiler_params=pltpu.CompilerParams(
            collective_id=0, has_side_effects=True, vmem_limit_bytes=32 * 1024 * 1024
        ),
        name="gather",
    )(*(pltpu.with_memory_space_constraint(x, pltpu.HBM) for x in arrays))


def tile_sum(s, n, w):
    ones = jnp.ones((16, 128), bf16)
    left = jnp.concatenate([s[0:16], s[0:16], s[16:32], ones], axis=0)
    dist2 = lax.dot_general(left, n, TN, preferred_element_type=f32)
    dist = pl.reciprocal(lax.rsqrt(lax.clamp(0.0, dist2, 1.0)), approx=True)
    inner = 1.0 - dist
    inner2 = inner * inner
    phi = (inner2 * inner2) * (0.25 + dist)
    hi = phi.astype(bf16)
    lo = (phi - hi.astype(f32)).astype(bf16)
    return lax.dot_general(
        jnp.concatenate([w, w], axis=1), jnp.concatenate([hi, lo], axis=0), NN,
        preferred_element_type=f32,
    )


def tiles_kernel(codes, n_ref, s_ref, w_ref, disp_ref, acc):
    total = codes[0, codes.shape[1] - 1]
    acc[...] = jnp.zeros_like(acc)

    def group(g, _):
        found = []
        for u in range(UNROLL):
            code = codes[0, g * UNROLL + u]
            node, surf = lax.shift_right_logical(code, 9), lax.bitwise_and(code, 511)
            found.append((node, tile_sum(s_ref[surf], n_ref[node], w_ref[surf])))
        for node, term in found:
            acc[node] += term
        return 0

    lax.fori_loop(0, lax.div(total + (UNROLL - 1), UNROLL), group, 0)
    row = rows_of((8, 128))
    for b in range(acc.shape[0]):
        one = acc[b, 0:8] + acc[b, 8:16]
        a, c = one[:, 0:128], one[:, 128:256]
        first = jnp.where(row == 0, pltpu.roll(a, 5, 0), pltpu.roll(a, 1, 0))
        second = jnp.where(row == 5, pltpu.roll(c, 3, 0), pltpu.roll(c, 2, 0))
        second = jnp.where(row == 4, pltpu.roll(c, 5, 0), second)
        disp_ref[:, b * 128:b * 128 + 128] = jnp.where(row < 4, first, second)


def tiles(codes, n_table, s_table, w_table):
    vmem = pl.BlockSpec(memory_space=pltpu.VMEM)
    node_blocks = n_table.shape[0]
    return pl.pallas_call(
        tiles_kernel,
        out_shape=jax.ShapeDtypeStruct((8, node_blocks * 128), f32),
        in_specs=[pl.BlockSpec(memory_space=pltpu.SMEM)] + [vmem] * 3,
        out_specs=vmem,
        scratch_shapes=[pltpu.VMEM((node_blocks, 16, 256), f32)],
        compiler_params=pltpu.CompilerParams(vmem_limit_bytes=32 * 1024 * 1024),
        name="tiles",
    )(codes, n_table, s_table, w_table)


def finish_kernel(disp_ref, nodes_ref, index_ref, count_ref, out_ref, ghost_ref,
                  part, outlist, inlist, xs, xr, gs, gr):
    inst, surf, half = lax.axis_index("inst"), lax.axis_index("surf"), lax.axis_index("half")
    n_inst, n_surf = 4, lax.axis_size("surf")
    after = (inst, (surf + 1) % n_surf, half)
    before = (inst, (surf + n_surf - 1) % n_surf, half)
    peers = [((inst + d) % n_inst, surf, half) for d in range(1, n_inst)]
    barrier = pltpu.get_barrier_semaphore()
    for to in peers + [after, before]:
        pl.semaphore_signal(barrier, inc=1, device_id=to, device_id_type=MESH)

    wide = disp_ref.shape[1]
    mid = wide // 2
    disp = disp_ref[...]
    both = disp + pltpu.roll(disp, 4, 0)
    part[0] = jnp.where(rows_of((8, mid)) < 4, both[:, :mid], both[:, mid:])
    pl.semaphore_wait(barrier, n_inst + 1)
    copies = [
        pltpu.make_async_remote_copy(
            src_ref=part.at[0], dst_ref=part.at[d], send_sem=xs.at[d - 1], recv_sem=xr.at[d - 1],
            device_id=peers[d - 1], device_id_type=MESH,
        )
        for d in range(1, n_inst)
    ]
    for c in copies:
        c.start()

    index = jnp.concatenate([index_ref[0, 0:1, :], index_ref[0, 1:2, :]], axis=1)
    slots = index.shape[1] // 2
    lane = lax.broadcasted_iota(jnp.int32, (8, 2 * slots), 1)
    live = lane < jnp.where(lane < slots, count_ref[0, 0], count_ref[0, 1] + slots)
    pick = (rows_of((128, 2 * slots)) == index % 128).astype(f32).astype(bf16)
    block = index // 128
    gap = jnp.zeros((1, wide), f32)
    nodes = nodes_ref[...]
    nodes8 = jnp.concatenate([nodes, gap, nodes, gap], axis=0)

    for c in copies:
        c.wait_recv()
    total = (part[0] + part[1] + part[2] + part[3]) * (1.0 / (2 * n_inst))
    swapped = pltpu.roll(total, 4, 0)
    low = rows_of((8, mid)) < 4
    spectral = jnp.concatenate([jnp.where(low, total, swapped), jnp.where(low, swapped, total)], axis=1)
    deformed = nodes8 + spectral + HARMONIC * (disp - spectral)
    for k in range(3):
        out_ref[k] = jnp.concatenate([deformed[k:k + 1], deformed[4 + k:5 + k]], axis=0)

    tall = jnp.concatenate([deformed[:, b * 128:b * 128 + 128] for b in range(wide // 128)], axis=0)
    picked = sum(lax.dot_general(piece, pick, NN, preferred_element_type=f32) for piece in split3(tall))
    chosen = jnp.zeros((8, 2 * slots), f32)
    for b in range(wide // 128):
        chosen += jnp.where(block == b, picked[b * 8:b * 8 + 8], 0.0)
    chosen = jnp.where(live, chosen, 0.0)
    outlist[...] = chosen
    lists = [
        pltpu.make_async_remote_copy(
            src_ref=outlist, dst_ref=inlist.at[e], send_sem=gs.at[e], recv_sem=gr.at[e],
            device_id=to, device_id_type=MESH,
        )
        for e, to in enumerate((before, after))
    ]
    for c in lists:
        c.start()
    for c in lists:
        c.wait_recv()
    lower = jnp.where(surf > 0, inlist[1], 0.0)
    upper = jnp.where(surf < n_surf - 1, inlist[0], 0.0)
    shown = jnp.concatenate([lower[:, slots:], upper[:, :slots]], axis=1)
    for k in range(3):
        ghost_ref[k] = jnp.concatenate([shown[k:k + 1], shown[4 + k:5 + k]], axis=0)
    for c in copies + lists:
        c.wait_send()


def finish(disp, nodes, bnd_index, bnd_count):
    vmem = pl.BlockSpec(memory_space=pltpu.VMEM)
    smem = pl.BlockSpec(memory_space=pltpu.SMEM)
    dma = pltpu.SemaphoreType.DMA
    wide, slots = nodes.shape[1], bnd_index.shape[2]
    return pl.pallas_call(
        finish_kernel,
        out_shape=(
            jax.ShapeDtypeStruct((3, 2, wide), f32),
            jax.ShapeDtypeStruct((3, 2, 2 * slots), f32),
        ),
        in_specs=[vmem, vmem, vmem, smem],
        out_specs=(vmem, vmem),
        scratch_shapes=[
            pltpu.VMEM((4, 8, wide // 2), f32),
            pltpu.VMEM((8, 2 * slots), f32),
            pltpu.VMEM((2, 8, 2 * slots), f32),
            dma((3,)), dma((3,)), dma((2,)), dma((2,)),
        ],
        compiler_params=pltpu.CompilerParams(
            collective_id=1, has_side_effects=True, vmem_limit_bytes=32 * 1024 * 1024
        ),
        name="finish",
    )(disp, nodes, bnd_index, bnd_count)


def shards(nodes, surf_coords, surf_weights, tile_node, tile_surf, tile_count, bnd_index, bnd_count):
    n_table, s_table, w_table, codes = gather(
        nodes,
        surf_coords.transpose(1, 0, 2),
        surf_weights.transpose(1, 0, 2),
        tile_node.transpose(0, 1, 3, 2),
        tile_surf.transpose(0, 1, 3, 2),
        tile_count,
    )
    disp = tiles(codes, n_table, s_table, w_table)
    out, ghosts = finish(disp, nodes, bnd_index, bnd_count)
    return out.transpose(1, 0, 2), ghosts.transpose(1, 0, 2)


def solution(mesh):
    in_specs = (
        P(None, ("surf", "half")),
        P("inst", None, "surf"),
        P("inst", None, "surf"),
        P("surf", "half", None, None),
        P("surf", "half", None, None),
        P("surf", "half", None),
        P(("surf", "half"), None, None),
        P(("surf", "half"), None),
    )
    out_specs = (P("inst", None, ("surf", "half")), P("inst", None, ("surf", "half")))
    return jax.shard_map(shards, mesh=mesh, in_specs=in_specs, out_specs=out_specs, check_vma=False)
```

```python
import functools

import jax
import jax.numpy as jnp
from jax import lax
from jax.experimental import pallas as pl
from jax.experimental.pallas import tpu as pltpu
from jax.sharding import PartitionSpec as P

RADIUS = 0.4
HARMONIC = 0.8
CENTRE = 0.25
UNROLL = 48
TAIL = 16

f32 = jnp.float32
bf16 = jnp.bfloat16
MESH = pl.DeviceIdType.MESH
NN = (((1,), (0,)), ((), ()))
TN = (((0,), (0,)), ((), ()))


def split3(x):
    a = x.astype(bf16)
    rest = x - a.astype(f32)
    b = rest.astype(bf16)
    c = (rest - b.astype(f32)).astype(bf16)
    return a, b, c


def rows_of(shape):
    return lax.broadcasted_iota(jnp.int32, shape, 0)


def node_tables(nodes_ref, n_ref):
    row = rows_of((8, 128))
    blocks = nodes_ref.shape[1] // 128

    def one(b, _):
        x = (nodes_ref[:, pl.ds(pl.multiple_of(b * 128, 128), 128)] - CENTRE) * (1.0 / RADIUS)
        sq = x * x
        p = sq[0:1] + sq[1:2] + sq[2:3]
        four = jnp.concatenate([-2.0 * x, jnp.ones((1, 128), f32)], axis=0)
        eight = jnp.concatenate([four, four], axis=0)
        left, right = jnp.where(row < 4, eight, 0.0), jnp.where(row < 4, 0.0, eight)
        wide = jnp.concatenate([left, right], axis=1)
        b0, b1, b2 = split3(wide)
        p0, p1, p2 = split3(jnp.concatenate([p, p], axis=1))
        zero = jnp.zeros((13, 256), f32)
        tail = jnp.concatenate([p0.astype(f32), p1.astype(f32), p2.astype(f32), zero], axis=0).astype(bf16)
        n_ref[b, 0:16] = jnp.concatenate([b0, b0], axis=0)
        n_ref[b, 16:32] = jnp.concatenate([b1, b1], axis=0)
        n_ref[b, 32:48] = jnp.concatenate([b2, b0], axis=0)
        n_ref[b, 48:64] = tail
        return 0

    lax.fori_loop(0, blocks, one, 0)


def surface_tables(held, j, s_ref, w_ref):
    raw = jnp.concatenate([held[j, 0], held[j, 1]], axis=0)
    rest = held[j, 2]
    row = rows_of(raw.shape)
    c = (raw - CENTRE) * (1.0 / RADIUS)
    sq = c * c
    q = pltpu.roll(sq, 1, 0) + pltpu.roll(sq, 2, 0) + pltpu.roll(sq, 3, 0)
    a0, a1, a2 = split3(jnp.where(row % 4 == 3, q, c))
    first = jnp.concatenate([a0, a1], axis=0)
    second = jnp.concatenate([a0, a2], axis=0)
    w = jnp.concatenate([rest, rest[3:4], rest[0:3]], axis=0)
    w = jnp.where(row % 4 == 3, raw, w) * 4.0
    hi = w.astype(bf16)
    both = jnp.concatenate([hi, (w - hi.astype(f32)).astype(bf16)], axis=0)
    per = c.shape[1] // 128
    for b in range(per):
        at = slice(b * 128, b * 128 + 128)
        s_ref[j * per + b, 0:16] = first[:, at]
        s_ref[j * per + b, 16:32] = second[:, at]
        w_ref[j * per + b] = both[:, at]


def compact(node_list, surf_list, counts, codes_ref, per, dummy):
    most, n = node_list.shape
    size = codes_ref.shape[1]
    lane = lax.broadcasted_iota(jnp.int32, (most, n), 1)
    code = node_list[...] * 512 + surf_list[...] + lane * per
    count = counts[...]
    wide = jnp.broadcast_to(count.astype(f32), (8, n)).astype(bf16)
    earlier = (rows_of((n, n)) < lax.broadcasted_iota(jnp.int32, (n, n), 1)).astype(f32).astype(bf16)
    base = lax.dot_general(wide, earlier, NN, preferred_element_type=f32)[0:1].astype(jnp.int32)
    slot = rows_of((most, n))
    dest = jnp.where(slot < count, base + slot, -1)
    place = lax.broadcasted_iota(jnp.int32, (most, size), 1)
    found = jnp.zeros((most, size), jnp.int32)
    for o in range(n):
        found += jnp.where(dest[:, o:o + 1] == place, code[:, o:o + 1], 0)
    total = (base + count)[:, n - 1:n]
    line = lax.broadcasted_iota(jnp.int32, (1, size), 1)
    listed = jnp.sum(found, axis=0, keepdims=True) + jnp.where(line >= total, dummy, 0)
    codes_ref[...] = jnp.where(line == size - 1, total, listed)


def gather_kernel(nodes_hbm, coords_hbm, weights_hbm, node_list_hbm, surf_list_hbm, counts_hbm,
                  n_ref, s_ref, w_ref, codes_ref,
                  held, nodes_in, coords_in, weights_in, node_list, surf_list, counts, local,
                  zs, zr, ys, yr, cs, cr):
    inst, surf, half = lax.axis_index("inst"), lax.axis_index("surf"), lax.axis_index("half")
    z, y_lo, core = surf // 4, (surf // 2) % 2, surf % 2
    ring = 8

    def at(zz, yy, cc):
        return (zz % ring) * 4 + yy * 2 + cc

    def along(d):
        return (inst, at(z + ring + d, y_lo, core), half)

    beside = (inst, at(z, 1 - y_lo, core), half)
    across = (inst, at(z, 1 - y_lo, core), 1 - half)
    twin = (inst, at(z, y_lo, 1 - core), half)

    barrier = pltpu.get_barrier_semaphore()
    for other in (along(1), along(-1), along(2), along(-2), beside, across, twin):
        pl.semaphore_signal(barrier, inc=1, device_id=other, device_id_type=MESH)
    pairs = (
        (coords_hbm, coords_in), (weights_hbm, weights_in), (nodes_hbm, nodes_in),
        (node_list_hbm.at[0, 0], node_list), (surf_list_hbm.at[0, 0], surf_list), (counts_hbm.at[0], counts),
    )
    loads = [pltpu.make_async_copy(src, dst, local.at[i]) for i, (src, dst) in enumerate(pairs)]
    for c in loads:
        c.start()
    per = coords_in.shape[2] // 128
    last = s_ref.shape[0] - 1
    s_ref[last] = jnp.zeros_like(s_ref[last])
    w_ref[last] = jnp.zeros_like(w_ref[last])
    mine = at(z, y_lo, core)
    loads[0].wait()
    loads[1].wait()
    c_in, w_in = coords_in, weights_in
    for i in range(2):
        held[mine, i] = jnp.concatenate([c_in[k, i:i + 1] for k in range(3)] + [w_in[0, i:i + 1]], axis=0)
    held[mine, 2] = jnp.concatenate([w_in[k, i:i + 1] for i in range(2) for k in (1, 2)], axis=0)

    mid = coords_in.shape[2] // 2
    low, high = pl.ds(0, mid), pl.ds(mid, mid)
    offsets = [0, -1, 1, -2, 2, -3, 3, 4]

    def copy(ref, send, recv, to):
        return pltpu.make_async_remote_copy(
            src_ref=ref, dst_ref=ref, send_sem=send, recv_sem=recv, device_id=to, device_id_type=MESH
        )

    def part(block, lanes=None):
        return held.at[block] if lanes is None else held.at[block, :, :, lanes]

    def own(d):
        return at(z + ring + d, y_lo, core)

    def other(d):
        return at(z + ring + d, 1 - y_lo, core)

    routes = {
        1: (1, 0, None), 2: (-1, 0, None), 3: (2, 0, None), 4: (-2, 0, None),
        5: (1, -2, None), 6: (-1, 2, None), 7: (2, -2, low), 0: (-2, 2, high),
    }

    def zcopy(r, arriving=False):
        step, origin, lanes = routes[r]
        block = own(origin - step) if arriving else own(origin)
        return copy(part(block, lanes), zs.at[r], zr.at[r], along(step))

    def ycopies(q, block):
        return (
            copy(part(block, low), ys.at[q], yr.at[q], beside),
            copy(part(block, high), ys.at[8 + q], yr.at[8 + q], across),
        )

    def ccopy(q, block):
        return copy(part(block), cs.at[q], cr.at[q], twin)

    sent = []

    def go(c):
        c.start()
        sent.append(c)

    def spread(q):
        for c in ycopies(q, own(offsets[q])):
            go(c)
        go(ccopy(q, own(offsets[q])))
        surface_tables(held, own(offsets[q]), s_ref, w_ref)

    def take_other(q):
        for c in ycopies(q, other(offsets[q])):
            c.wait_recv()
        go(ccopy(8 + q, other(offsets[q])))
        surface_tables(held, other(offsets[q]), s_ref, w_ref)

    pl.semaphore_wait(barrier, 7)
    for r in (1, 2, 3, 4):
        go(zcopy(r))
    spread(0)
    for c in loads[2:]:
        c.wait()
    node_tables(nodes_in, n_ref)
    compact(node_list, surf_list, counts, codes_ref, per, last)

    zcopy(1, True).wait_recv()
    spread(1)
    zcopy(2, True).wait_recv()
    spread(2)
    take_other(0)
    zcopy(3, True).wait_recv()
    go(zcopy(5))
    go(zcopy(7))
    spread(3)
    zcopy(4, True).wait_recv()
    go(zcopy(6))
    go(zcopy(0))
    spread(4)
    for q in (1, 2, 3, 4):
        take_other(q)
    zcopy(5, True).wait_recv()
    spread(5)
    zcopy(6, True).wait_recv()
    spread(6)
    zcopy(7, True).wait_recv()
    zcopy(0, True).wait_recv()
    spread(7)
    for q in (5, 6, 7):
        take_other(q)
    for q in range(16):
        block = at(z + ring + offsets[q % 8], y_lo if q < 8 else 1 - y_lo, 1 - core)
        ccopy(q, block).wait_recv()
        surface_tables(held, block, s_ref, w_ref)
    for c in sent:
        c.wait_send()


def gather(nodes, coords, weights, tile_node, tile_surf, tile_count):
    arrays = (nodes, coords, weights, tile_node, tile_surf, tile_count)
    n_surf = lax.axis_size("surf")
    points = coords.shape[2]
    blocks = n_surf * points // 128
    most, n = tile_node.shape[2:]
    size = most * n + 128
    vmem = pl.BlockSpec(memory_space=pltpu.VMEM)
    dma = pltpu.SemaphoreType.DMA
    return pl.pallas_call(
        gather_kernel,
        out_shape=(
            jax.ShapeDtypeStruct((nodes.shape[1] // 128, 64, 256), bf16),
            jax.ShapeDtypeStruct((blocks + 1, 32, 128), bf16),
            jax.ShapeDtypeStruct((blocks + 1, 16, 128), bf16),
            jax.ShapeDtypeStruct((1, size), jnp.int32),
        ),
        in_specs=[pl.BlockSpec(memory_space=pltpu.HBM)] * 6,
        out_specs=(vmem,) * 4,
        scratch_shapes=[
            pltpu.VMEM((n_surf, 3, 4, points), f32),
            pltpu.VMEM(nodes.shape, f32),
            pltpu.VMEM(coords.shape, f32),
            pltpu.VMEM(weights.shape, f32),
            pltpu.VMEM((most, n), jnp.int32),
            pltpu.VMEM((most, n), jnp.int32),
            pltpu.VMEM((1, n), jnp.int32),
            dma((6,)),
            dma((8,)), dma((8,)), dma((16,)), dma((16,)), dma((16,)), dma((16,)),
        ],
        compiler_params=pltpu.CompilerParams(
            collective_id=0, has_side_effects=True, vmem_limit_bytes=32 * 1024 * 1024
        ),
        name="gather",
    )(*(pltpu.with_memory_space_constraint(x, pltpu.HBM) for x in arrays))


def tile_sum(s, n, w):
    ones = jnp.ones((16, 128), bf16)
    left = jnp.concatenate([s[0:16], s[0:16], s[16:32], ones], axis=0)
    dist2 = lax.dot_general(left, n, TN, preferred_element_type=f32)
    dist = pl.reciprocal(lax.rsqrt(lax.clamp(0.0, dist2, 1.0)), approx=True)
    inner = 1.0 - dist
    inner2 = inner * inner
    phi = (inner2 * inner2) * (0.25 + dist)
    hi = phi.astype(bf16)
    lo = (phi - hi.astype(f32)).astype(bf16)
    return lax.dot_general(
        jnp.concatenate([w, w], axis=1), jnp.concatenate([hi, lo], axis=0), NN,
        preferred_element_type=f32,
    )


def tiles_kernel(codes, n_ref, s_ref, w_ref, disp_ref, acc):
    total = codes[0, codes.shape[1] - 1]
    acc[...] = jnp.zeros_like(acc)

    def group(first, many):
        found = []
        for u in range(many):
            code = codes[0, first + u]
            node, surf = lax.shift_right_logical(code, 9), lax.bitwise_and(code, 511)
            found.append((node, tile_sum(s_ref[surf], n_ref[node], w_ref[surf])))
        for node, term in found:
            acc[node] += term
        return 0

    full = lax.div(total, UNROLL)
    lax.fori_loop(0, full, lambda g, _: group(g * UNROLL, UNROLL), 0)
    rest = full * UNROLL
    lax.fori_loop(0, lax.div(total - rest + (TAIL - 1), TAIL), lambda g, _: group(rest + g * TAIL, TAIL), 0)
    row = rows_of((8, 128))
    for b in range(acc.shape[0]):
        one = acc[b, 0:8] + acc[b, 8:16]
        a, c = one[:, 0:128], one[:, 128:256]
        first = jnp.where(row == 0, pltpu.roll(a, 5, 0), pltpu.roll(a, 1, 0))
        second = jnp.where(row == 5, pltpu.roll(c, 3, 0), pltpu.roll(c, 2, 0))
        second = jnp.where(row == 4, pltpu.roll(c, 5, 0), second)
        disp_ref[:, b * 128:b * 128 + 128] = jnp.where(row < 4, first, second)


def tiles(codes, n_table, s_table, w_table):
    vmem = pl.BlockSpec(memory_space=pltpu.VMEM)
    node_blocks = n_table.shape[0]
    return pl.pallas_call(
        tiles_kernel,
        out_shape=jax.ShapeDtypeStruct((8, node_blocks * 128), f32),
        in_specs=[pl.BlockSpec(memory_space=pltpu.SMEM)] + [vmem] * 3,
        out_specs=vmem,
        scratch_shapes=[pltpu.VMEM((node_blocks, 16, 256), f32)],
        compiler_params=pltpu.CompilerParams(vmem_limit_bytes=32 * 1024 * 1024),
        name="tiles",
    )(codes, n_table, s_table, w_table)


def finish_kernel(disp_ref, nodes_ref, index_ref, count_ref, out_ref, ghost_ref,
                  part, outlist, inlist, xs, xr, gs, gr):
    inst, surf, half = lax.axis_index("inst"), lax.axis_index("surf"), lax.axis_index("half")
    n_inst, n_surf = 4, lax.axis_size("surf")
    peers = [((inst + d) % n_inst, surf, half) for d in range(1, n_inst)]
    ends = [(surf + n_surf - 1) % n_surf, (surf + 1) % n_surf]
    others = [((inst + d) % n_inst, ends[e], half) for e in range(2) for d in range(n_inst)]
    barrier = pltpu.get_barrier_semaphore()
    for to in peers + others:
        pl.semaphore_signal(barrier, inc=1, device_id=to, device_id_type=MESH)

    wide = disp_ref.shape[1]
    mid = wide // 2
    disp = disp_ref[...]
    both = disp + pltpu.roll(disp, 4, 0)
    part[0] = jnp.where(rows_of((8, mid)) < 4, both[:, :mid], both[:, mid:])
    pl.semaphore_wait(barrier, 3 * n_inst - 1)
    copies = [
        pltpu.make_async_remote_copy(
            src_ref=part.at[0], dst_ref=part.at[d], send_sem=xs.at[d - 1], recv_sem=xr.at[d - 1],
            device_id=peers[d - 1], device_id_type=MESH,
        )
        for d in range(1, n_inst)
    ]
    for c in copies:
        c.start()

    index = jnp.concatenate([index_ref[0, 0:1, :], index_ref[0, 1:2, :]], axis=1)
    slots = index.shape[1] // 2
    lane = lax.broadcasted_iota(jnp.int32, (8, 2 * slots), 1)
    live = lane < jnp.where(lane < slots, count_ref[0, 0], count_ref[0, 1] + slots)
    pick = (rows_of((128, 2 * slots)) == index % 128).astype(f32).astype(bf16)
    block = index // 128
    gap = jnp.zeros((1, wide), f32)
    nodes = nodes_ref[...]
    nodes8 = jnp.concatenate([nodes, gap, nodes, gap], axis=0)

    def picked(x):
        tall = jnp.concatenate([x[:, b * 128:b * 128 + 128] for b in range(wide // 128)], axis=0)
        lanes = sum(lax.dot_general(piece, pick, NN, preferred_element_type=f32) for piece in split3(tall))
        chosen = jnp.zeros((8, 2 * slots), f32)
        for b in range(wide // 128):
            chosen += jnp.where(block == b, lanes[b * 8:b * 8 + 8], 0.0)
        return chosen

    outlist[0:8] = picked(disp)
    outlist[8:16] = picked(nodes8)
    outlist[16:24] = jnp.where(live, 1.0, 0.0)
    lists = [
        pltpu.make_async_remote_copy(
            src_ref=outlist, dst_ref=inlist.at[i], send_sem=gs.at[i], recv_sem=gr.at[i],
            device_id=to, device_id_type=MESH,
        )
        for i, to in enumerate(others)
    ]
    for c in lists:
        c.start()

    for c in copies:
        c.wait_recv()
    total = (part[0] + part[1] + part[2] + part[3]) * (1.0 / (2 * n_inst))
    swapped = pltpu.roll(total, 4, 0)
    low = rows_of((8, mid)) < 4
    spectral = jnp.concatenate([jnp.where(low, total, swapped), jnp.where(low, swapped, total)], axis=1)
    deformed = nodes8 + spectral + HARMONIC * (disp - spectral)
    for k in range(3):
        out_ref[k] = jnp.concatenate([deformed[k:k + 1], deformed[4 + k:5 + k]], axis=0)

    for c in lists:
        c.wait_recv()

    def received(e):
        first = e * n_inst
        moved = inlist[first, 0:8]
        total = moved
        for d in range(1, n_inst):
            total += inlist[first + d, 0:8]
        mean = (total + pltpu.roll(total, 4, 0)) * (1.0 / (2 * n_inst))
        value = inlist[first, 8:16] + mean + HARMONIC * (moved - mean)
        return jnp.where(inlist[first, 16:24] > 0.5, value, 0.0)

    lower = jnp.where(surf > 0, received(1), 0.0)
    upper = jnp.where(surf < n_surf - 1, received(0), 0.0)
    shown = jnp.concatenate([lower[:, slots:], upper[:, :slots]], axis=1)
    for k in range(3):
        ghost_ref[k] = jnp.concatenate([shown[k:k + 1], shown[4 + k:5 + k]], axis=0)
    for c in copies + lists:
        c.wait_send()


def finish(disp, nodes, bnd_index, bnd_count):
    vmem = pl.BlockSpec(memory_space=pltpu.VMEM)
    smem = pl.BlockSpec(memory_space=pltpu.SMEM)
    dma = pltpu.SemaphoreType.DMA
    wide, slots = nodes.shape[1], bnd_index.shape[2]
    return pl.pallas_call(
        finish_kernel,
        out_shape=(
            jax.ShapeDtypeStruct((3, 2, wide), f32),
            jax.ShapeDtypeStruct((3, 2, 2 * slots), f32),
        ),
        in_specs=[vmem, vmem, vmem, smem],
        out_specs=(vmem, vmem),
        scratch_shapes=[
            pltpu.VMEM((4, 8, wide // 2), f32),
            pltpu.VMEM((24, 2 * slots), f32),
            pltpu.VMEM((8, 24, 2 * slots), f32),
            dma((3,)), dma((3,)), dma((8,)), dma((8,)),
        ],
        compiler_params=pltpu.CompilerParams(
            collective_id=1, has_side_effects=True, vmem_limit_bytes=32 * 1024 * 1024
        ),
        name="finish",
    )(disp, nodes, bnd_index, bnd_count)


def shards(nodes, surf_coords, surf_weights, tile_node, tile_surf, tile_count, bnd_index, bnd_count):
    n_table, s_table, w_table, codes = gather(
        nodes,
        surf_coords.transpose(1, 0, 2),
        surf_weights.transpose(1, 0, 2),
        tile_node.transpose(0, 1, 3, 2),
        tile_surf.transpose(0, 1, 3, 2),
        tile_count,
    )
    disp = tiles(codes, n_table, s_table, w_table)
    out, ghosts = finish(disp, nodes, bnd_index, bnd_count)
    return out.transpose(1, 0, 2), ghosts.transpose(1, 0, 2)


def solution(mesh):
    in_specs = (
        P(None, ("surf", "half")),
        P("inst", None, "surf"),
        P("inst", None, "surf"),
        P("surf", "half", None, None),
        P("surf", "half", None, None),
        P("surf", "half", None),
        P(("surf", "half"), None, None),
        P(("surf", "half"), None),
    )
    out_specs = (P("inst", None, ("surf", "half")), P("inst", None, ("surf", "half")))
    return jax.shard_map(shards, mesh=mesh, in_specs=in_specs, out_specs=out_specs, check_vma=False)
```

```python
import functools

import jax
import jax.numpy as jnp
from jax import lax
from jax.experimental import pallas as pl
from jax.experimental.pallas import tpu as pltpu
from jax.sharding import PartitionSpec as P

RADIUS = 0.4
HARMONIC = 0.8
CENTRE = 0.25
UNROLL = 48
TAIL = 16
EARLY = 24
BATCHES = 4
PER_STEP = 12

f32 = jnp.float32
bf16 = jnp.bfloat16
MESH = pl.DeviceIdType.MESH
NN = (((1,), (0,)), ((), ()))
TN = (((0,), (0,)), ((), ()))


def split3(x):
    a = x.astype(bf16)
    rest = x - a.astype(f32)
    b = rest.astype(bf16)
    c = (rest - b.astype(f32)).astype(bf16)
    return a, b, c


def rows_of(shape):
    return lax.broadcasted_iota(jnp.int32, shape, 0)


def node_tables(nodes_ref, n_ref):
    row = rows_of((8, 128))
    blocks = nodes_ref.shape[1] // 128

    def one(b, _):
        x = (nodes_ref[:, pl.ds(pl.multiple_of(b * 128, 128), 128)] - CENTRE) * (1.0 / RADIUS)
        sq = x * x
        p = sq[0:1] + sq[1:2] + sq[2:3]
        four = jnp.concatenate([-2.0 * x, jnp.ones((1, 128), f32)], axis=0)
        eight = jnp.concatenate([four, four], axis=0)
        left, right = jnp.where(row < 4, eight, 0.0), jnp.where(row < 4, 0.0, eight)
        wide = jnp.concatenate([left, right], axis=1)
        b0, b1, b2 = split3(wide)
        p0, p1, p2 = split3(jnp.concatenate([p, p], axis=1))
        zero = jnp.zeros((13, 256), f32)
        tail = jnp.concatenate([p0.astype(f32), p1.astype(f32), p2.astype(f32), zero], axis=0).astype(bf16)
        n_ref[b, 0:16] = jnp.concatenate([b0, b0], axis=0)
        n_ref[b, 16:32] = jnp.concatenate([b1, b1], axis=0)
        n_ref[b, 32:48] = jnp.concatenate([b2, b0], axis=0)
        n_ref[b, 48:64] = tail
        return 0

    lax.fori_loop(0, blocks, one, 0)


def surface_tables(held, j, s_ref, w_ref):
    raw = jnp.concatenate([held[j, 0], held[j, 1]], axis=0)
    rest = held[j, 2]
    row = rows_of(raw.shape)
    c = (raw - CENTRE) * (1.0 / RADIUS)
    sq = c * c
    q = pltpu.roll(sq, 1, 0) + pltpu.roll(sq, 2, 0) + pltpu.roll(sq, 3, 0)
    a0, a1, a2 = split3(jnp.where(row % 4 == 3, q, c))
    first = jnp.concatenate([a0, a1], axis=0)
    second = jnp.concatenate([a0, a2], axis=0)
    w = jnp.concatenate([rest, rest[3:4], rest[0:3]], axis=0)
    w = jnp.where(row % 4 == 3, raw, w) * 4.0
    hi = w.astype(bf16)
    both = jnp.concatenate([hi, (w - hi.astype(f32)).astype(bf16)], axis=0)
    per = c.shape[1] // 128
    for b in range(per):
        at = slice(b * 128, b * 128 + 128)
        s_ref[j * per + b, 0:16] = first[:, at]
        s_ref[j * per + b, 16:32] = second[:, at]
        w_ref[j * per + b] = both[:, at]


def tile_sum(s, n, w):
    ones = jnp.ones((16, 128), bf16)
    left = jnp.concatenate([s[0:16], s[0:16], s[16:32], ones], axis=0)
    dist2 = lax.dot_general(left, n, TN, preferred_element_type=f32)
    dist = pl.reciprocal(lax.rsqrt(lax.clamp(0.0, dist2, 1.0)), approx=True)
    inner = 1.0 - dist
    inner2 = inner * inner
    phi = (inner2 * inner2) * (0.25 + dist)
    hi = phi.astype(bf16)
    lo = (phi - hi.astype(f32)).astype(bf16)
    return lax.dot_general(
        jnp.concatenate([w, w], axis=1), jnp.concatenate([hi, lo], axis=0), NN,
        preferred_element_type=f32,
    )


def compact(node_list, surf_list, counts, codes_ref, per, dummy, z, y_lo, ring):
    most, n = node_list.shape
    size = codes_ref.shape[1]
    lane = lax.broadcasted_iota(jnp.int32, (most, n), 1)
    code = node_list[...] * 512 + surf_list[...] + lane * per
    count = counts[...]
    wide = jnp.broadcast_to(count.astype(f32), (8, n)).astype(bf16)

    def apart(o):
        d = lax.rem(o // 4 + ring - z, ring)
        near = jnp.where(lax.rem(o, 4) // 2 == y_lo, 0, 1)
        return jnp.where(d == 0, near, jnp.where(d == 1, 2, jnp.where(d == ring - 1, 2, 3)))

    def key(o):
        return o + apart(o) * n

    earlier = key(rows_of((n, n))) < key(lax.broadcasted_iota(jnp.int32, (n, n), 1))
    earlier = earlier.astype(f32).astype(bf16)
    base = lax.dot_general(wide, earlier, NN, preferred_element_type=f32)[0:1].astype(jnp.int32)
    slot = rows_of((most, n))
    dest = jnp.where(slot < count, base + slot, -1)
    place = lax.broadcasted_iota(jnp.int32, (most, size), 1)
    found = jnp.zeros((most, size), jnp.int32)
    for o in range(n):
        found += jnp.where(dest[:, o:o + 1] == place, code[:, o:o + 1], 0)
    far = apart(lax.broadcasted_iota(jnp.int32, (1, n), 1))

    def within(d):
        held = jnp.where(far <= d, count, 0).astype(f32)
        return jnp.sum(held, axis=1, keepdims=True).astype(jnp.int32)

    total = within(3)
    line = lax.broadcasted_iota(jnp.int32, (1, size), 1)
    listed = jnp.sum(found, axis=0, keepdims=True) + jnp.where(line >= total, dummy, 0)
    for d in range(4):
        listed = jnp.where(line == size - 4 + d, within(d), listed)
    codes_ref[...] = listed


def gather_kernel(nodes_hbm, coords_hbm, weights_hbm, node_list_hbm, surf_list_hbm, counts_hbm,
                  n_ref, s_ref, w_ref, codes_ref, terms_ref, early_ref,
                  held, nodes_in, coords_in, weights_in, node_list, surf_list, counts, codes, local,
                  zs, zr, ys, yr, cs, cr):
    inst, surf, half = lax.axis_index("inst"), lax.axis_index("surf"), lax.axis_index("half")
    z, y_lo, core = surf // 4, (surf // 2) % 2, surf % 2
    ring = 8

    def at(zz, yy, cc):
        return (zz % ring) * 4 + yy * 2 + cc

    def along(d):
        return (inst, at(z + ring + d, y_lo, core), half)

    beside = (inst, at(z, 1 - y_lo, core), half)
    across = (inst, at(z, 1 - y_lo, core), 1 - half)
    twin = (inst, at(z, y_lo, 1 - core), half)

    barrier = pltpu.get_barrier_semaphore()
    for other in (along(1), along(-1), along(2), along(-2), beside, across, twin):
        pl.semaphore_signal(barrier, inc=1, device_id=other, device_id_type=MESH)
    pairs = (
        (coords_hbm, coords_in), (weights_hbm, weights_in), (nodes_hbm, nodes_in),
        (node_list_hbm.at[0, 0], node_list), (surf_list_hbm.at[0, 0], surf_list), (counts_hbm.at[0], counts),
    )
    loads = [pltpu.make_async_copy(src, dst, local.at[i]) for i, (src, dst) in enumerate(pairs)]
    for c in loads:
        c.start()
    per = coords_in.shape[2] // 128
    last = s_ref.shape[0] - 1
    s_ref[last] = jnp.zeros_like(s_ref[last])
    w_ref[last] = jnp.zeros_like(w_ref[last])
    mine = at(z, y_lo, core)
    loads[0].wait()
    loads[1].wait()
    c_in, w_in = coords_in, weights_in
    for i in range(2):
        held[mine, i] = jnp.concatenate([c_in[k, i:i + 1] for k in range(3)] + [w_in[0, i:i + 1]], axis=0)
    held[mine, 2] = jnp.concatenate([w_in[k, i:i + 1] for i in range(2) for k in (1, 2)], axis=0)

    mid = coords_in.shape[2] // 2
    low, high = pl.ds(0, mid), pl.ds(mid, mid)
    offsets = [0, -1, 1, -2, 2, -3, 3, 4]

    def copy(ref, send, recv, to):
        return pltpu.make_async_remote_copy(
            src_ref=ref, dst_ref=ref, send_sem=send, recv_sem=recv, device_id=to, device_id_type=MESH
        )

    def part(block, lanes=None):
        return held.at[block] if lanes is None else held.at[block, :, :, lanes]

    def own(d):
        return at(z + ring + d, y_lo, core)

    def other(d):
        return at(z + ring + d, 1 - y_lo, core)

    routes = {
        1: (1, 0, None), 2: (-1, 0, None), 3: (2, 0, None), 4: (-2, 0, None),
        5: (1, -2, None), 6: (-1, 2, None), 7: (2, -2, low), 0: (-2, 2, high),
    }

    def zcopy(r, arriving=False):
        step, origin, lanes = routes[r]
        block = own(origin - step) if arriving else own(origin)
        return copy(part(block, lanes), zs.at[r], zr.at[r], along(step))

    def ycopies(q, block):
        return (
            copy(part(block, low), ys.at[q], yr.at[q], beside),
            copy(part(block, high), ys.at[8 + q], yr.at[8 + q], across),
        )

    def ccopy(q, block):
        return copy(part(block), cs.at[q], cr.at[q], twin)

    sent = []

    def go(c):
        c.start()
        sent.append(c)

    def spread(q):
        for c in ycopies(q, own(offsets[q])):
            go(c)
        go(ccopy(q, own(offsets[q])))
        surface_tables(held, own(offsets[q]), s_ref, w_ref)

    def take_other(q):
        for c in ycopies(q, other(offsets[q])):
            c.wait_recv()
        go(ccopy(8 + q, other(offsets[q])))
        surface_tables(held, other(offsets[q]), s_ref, w_ref)

    pl.semaphore_wait(barrier, 7)
    for r in (1, 2, 3, 4):
        go(zcopy(r))
    spread(0)
    for c in loads[2:]:
        c.wait()
    node_tables(nodes_in, n_ref)
    compact(node_list, surf_list, counts, codes_ref, per, last, z, y_lo, ring)
    listing = pltpu.make_async_copy(codes_ref, codes, local.at[6])
    listing.start()
    size = codes_ref.shape[1]

    def batch(b, reach, start):
        limit = codes[0, size - 4 + reach]
        for u in range(EARLY):
            code = codes[0, jnp.clip(start + u, 0, size - 1)]
            code = jnp.where(start + u < limit, code, last)
            node = jnp.clip(lax.shift_right_logical(code, 9), 0, n_ref.shape[0] - 1)
            surf_block = jnp.clip(lax.bitwise_and(code, 511), 0, last)
            early_ref[0, b * EARLY + u] = code
            terms_ref[b * EARLY + u] = tile_sum(s_ref[surf_block], n_ref[node], w_ref[surf_block])
        return jnp.minimum(start + EARLY, limit)

    def take_twin(q):
        block = at(z + ring + offsets[q % 8], y_lo if q < 8 else 1 - y_lo, 1 - core)
        ccopy(q, block).wait_recv()
        surface_tables(held, block, s_ref, w_ref)

    zcopy(1, True).wait_recv()
    spread(1)
    zcopy(2, True).wait_recv()
    spread(2)
    take_other(0)
    take_twin(0)
    listing.wait()
    start = batch(0, 0, 0)
    zcopy(3, True).wait_recv()
    go(zcopy(5))
    go(zcopy(7))
    zcopy(4, True).wait_recv()
    go(zcopy(6))
    go(zcopy(0))
    spread(3)
    spread(4)
    take_twin(8)
    take_other(1)
    take_other(2)
    start = batch(1, 1, start)
    take_other(3)
    take_other(4)
    zcopy(5, True).wait_recv()
    spread(5)
    zcopy(6, True).wait_recv()
    spread(6)
    zcopy(7, True).wait_recv()
    zcopy(0, True).wait_recv()
    spread(7)
    for q in (1, 2, 9, 10):
        take_twin(q)
    start = batch(2, 2, start)
    for q in (5, 6, 7):
        take_other(q)
    for q in (3, 4, 11, 12):
        take_twin(q)
    start = batch(3, 2, start)
    early_ref[0, early_ref.shape[1] - 1] = start
    early_ref[0, EARLY * BATCHES] = last
    terms_ref[EARLY * BATCHES] = jnp.zeros((16, 256), f32)
    for q in (5, 6, 7, 13, 14, 15):
        take_twin(q)
    for c in sent:
        c.wait_send()


def gather(nodes, coords, weights, tile_node, tile_surf, tile_count):
    arrays = (nodes, coords, weights, tile_node, tile_surf, tile_count)
    n_surf = lax.axis_size("surf")
    points = coords.shape[2]
    blocks = n_surf * points // 128
    most, n = tile_node.shape[2:]
    size = most * n + 128
    vmem = pl.BlockSpec(memory_space=pltpu.VMEM)
    dma = pltpu.SemaphoreType.DMA
    return pl.pallas_call(
        gather_kernel,
        out_shape=(
            jax.ShapeDtypeStruct((nodes.shape[1] // 128, 64, 256), bf16),
            jax.ShapeDtypeStruct((blocks + 1, 32, 128), bf16),
            jax.ShapeDtypeStruct((blocks + 1, 16, 128), bf16),
            jax.ShapeDtypeStruct((1, size), jnp.int32),
            jax.ShapeDtypeStruct((EARLY * BATCHES + 1, 16, 256), f32),
            jax.ShapeDtypeStruct((1, 128), jnp.int32),
        ),
        in_specs=[pl.BlockSpec(memory_space=pltpu.HBM)] * 6,
        out_specs=(vmem,) * 5 + (pl.BlockSpec(memory_space=pltpu.SMEM),),
        scratch_shapes=[
            pltpu.VMEM((n_surf, 3, 4, points), f32),
            pltpu.VMEM(nodes.shape, f32),
            pltpu.VMEM(coords.shape, f32),
            pltpu.VMEM(weights.shape, f32),
            pltpu.VMEM((most, n), jnp.int32),
            pltpu.VMEM((most, n), jnp.int32),
            pltpu.VMEM((1, n), jnp.int32),
            pltpu.SMEM((1, size), jnp.int32),
            dma((7,)),
            dma((8,)), dma((8,)), dma((16,)), dma((16,)), dma((16,)), dma((16,)),
        ],
        compiler_params=pltpu.CompilerParams(
            collective_id=0, has_side_effects=True, vmem_limit_bytes=32 * 1024 * 1024
        ),
        name="gather",
    )(*(pltpu.with_memory_space_constraint(x, pltpu.HBM) for x in arrays))


def tiles_kernel(codes, early, n_ref, s_ref, w_ref, terms_ref, disp_ref, acc):
    total = codes[0, codes.shape[1] - 1]
    begin = early[0, early.shape[1] - 1]
    acc[...] = jnp.zeros_like(acc)
    given = terms_ref.shape[0] - 1

    def given_term(k):
        return lax.shift_right_logical(early[0, k], 9), terms_ref[k]

    def group(first, many, taken=None):
        found = []
        if taken is not None:
            found += [given_term(jnp.minimum(taken + j, given)) for j in range(PER_STEP)]
        for u in range(many):
            code = codes[0, first + u]
            node, surf = lax.shift_right_logical(code, 9), lax.bitwise_and(code, 511)
            found.append((node, tile_sum(s_ref[surf], n_ref[node], w_ref[surf])))
        for node, term in found:
            acc[node] += term
        return 0

    full = lax.div(total - begin, UNROLL)
    lax.fori_loop(0, full, lambda g, _: group(begin + g * UNROLL, UNROLL, g * PER_STEP), 0)

    def add_given(k, _):
        node, term = given_term(k)
        acc[node] += term
        return 0

    lax.fori_loop(jnp.minimum(full * PER_STEP, given), given, add_given, 0)
    rest = begin + full * UNROLL
    lax.fori_loop(0, lax.div(total - rest + (TAIL - 1), TAIL), lambda g, _: group(rest + g * TAIL, TAIL), 0)
    row = rows_of((8, 128))
    for b in range(acc.shape[0]):
        one = acc[b, 0:8] + acc[b, 8:16]
        a, c = one[:, 0:128], one[:, 128:256]
        first = jnp.where(row == 0, pltpu.roll(a, 5, 0), pltpu.roll(a, 1, 0))
        second = jnp.where(row == 5, pltpu.roll(c, 3, 0), pltpu.roll(c, 2, 0))
        second = jnp.where(row == 4, pltpu.roll(c, 5, 0), second)
        disp_ref[:, b * 128:b * 128 + 128] = jnp.where(row < 4, first, second)


def tiles(codes, n_table, s_table, w_table, terms, early):
    vmem = pl.BlockSpec(memory_space=pltpu.VMEM)
    smem = pl.BlockSpec(memory_space=pltpu.SMEM)
    node_blocks = n_table.shape[0]
    return pl.pallas_call(
        tiles_kernel,
        out_shape=jax.ShapeDtypeStruct((8, node_blocks * 128), f32),
        in_specs=[smem] * 2 + [vmem] * 4,
        out_specs=vmem,
        scratch_shapes=[pltpu.VMEM((node_blocks, 16, 256), f32)],
        compiler_params=pltpu.CompilerParams(vmem_limit_bytes=32 * 1024 * 1024),
        name="tiles",
    )(codes, early, n_table, s_table, w_table, terms)


def finish_kernel(disp_ref, nodes_ref, index_ref, count_ref, out_ref, ghost_ref,
                  part, outlist, inlist, xs, xr, gs, gr):
    inst, surf, half = lax.axis_index("inst"), lax.axis_index("surf"), lax.axis_index("half")
    n_inst, n_surf = 4, lax.axis_size("surf")
    peers = [((inst + d) % n_inst, surf, half) for d in range(1, n_inst)]
    ends = [(surf + n_surf - 1) % n_surf, (surf + 1) % n_surf]
    others = [((inst + d) % n_inst, ends[e], half) for e in range(2) for d in range(n_inst)]
    barrier = pltpu.get_barrier_semaphore()
    for to in peers + others:
        pl.semaphore_signal(barrier, inc=1, device_id=to, device_id_type=MESH)

    wide = disp_ref.shape[1]
    mid = wide // 2
    disp = disp_ref[...]
    both = disp + pltpu.roll(disp, 4, 0)
    part[0] = jnp.where(rows_of((8, mid)) < 4, both[:, :mid], both[:, mid:])
    pl.semaphore_wait(barrier, 3 * n_inst - 1)
    copies = [
        pltpu.make_async_remote_copy(
            src_ref=part.at[0], dst_ref=part.at[d], send_sem=xs.at[d - 1], recv_sem=xr.at[d - 1],
            device_id=peers[d - 1], device_id_type=MESH,
        )
        for d in range(1, n_inst)
    ]
    for c in copies:
        c.start()

    index = jnp.concatenate([index_ref[0, 0:1, :], index_ref[0, 1:2, :]], axis=1)
    slots = index.shape[1] // 2
    lane = lax.broadcasted_iota(jnp.int32, (8, 2 * slots), 1)
    live = lane < jnp.where(lane < slots, count_ref[0, 0], count_ref[0, 1] + slots)
    pick = (rows_of((128, 2 * slots)) == index % 128).astype(f32).astype(bf16)
    block = index // 128
    gap = jnp.zeros((1, wide), f32)
    nodes = nodes_ref[...]
    nodes8 = jnp.concatenate([nodes, gap, nodes, gap], axis=0)

    def picked(x):
        tall = jnp.concatenate([x[:, b * 128:b * 128 + 128] for b in range(wide // 128)], axis=0)
        lanes = sum(lax.dot_general(piece, pick, NN, preferred_element_type=f32) for piece in split3(tall))
        chosen = jnp.zeros((8, 2 * slots), f32)
        for b in range(wide // 128):
            chosen += jnp.where(block == b, lanes[b * 8:b * 8 + 8], 0.0)
        return chosen

    outlist[0:8] = picked(disp)
    outlist[8:16] = picked(nodes8)
    outlist[16:24] = jnp.where(live, 1.0, 0.0)
    lists = [
        pltpu.make_async_remote_copy(
            src_ref=outlist, dst_ref=inlist.at[i], send_sem=gs.at[i], recv_sem=gr.at[i],
            device_id=to, device_id_type=MESH,
        )
        for i, to in enumerate(others)
    ]
    for c in lists:
        c.start()

    for c in copies:
        c.wait_recv()
    total = (part[0] + part[1] + part[2] + part[3]) * (1.0 / (2 * n_inst))
    swapped = pltpu.roll(total, 4, 0)
    low = rows_of((8, mid)) < 4
    spectral = jnp.concatenate([jnp.where(low, total, swapped), jnp.where(low, swapped, total)], axis=1)
    deformed = nodes8 + spectral + HARMONIC * (disp - spectral)
    for k in range(3):
        out_ref[k] = jnp.concatenate([deformed[k:k + 1], deformed[4 + k:5 + k]], axis=0)

    for c in lists:
        c.wait_recv()

    def received(e):
        first = e * n_inst
        moved = inlist[first, 0:8]
        total = moved
        for d in range(1, n_inst):
            total += inlist[first + d, 0:8]
        mean = (total + pltpu.roll(total, 4, 0)) * (1.0 / (2 * n_inst))
        value = inlist[first, 8:16] + mean + HARMONIC * (moved - mean)
        return jnp.where(inlist[first, 16:24] > 0.5, value, 0.0)

    lower = jnp.where(surf > 0, received(1), 0.0)
    upper = jnp.where(surf < n_surf - 1, received(0), 0.0)
    shown = jnp.concatenate([lower[:, slots:], upper[:, :slots]], axis=1)
    for k in range(3):
        ghost_ref[k] = jnp.concatenate([shown[k:k + 1], shown[4 + k:5 + k]], axis=0)
    for c in copies + lists:
        c.wait_send()


def finish(disp, nodes, bnd_index, bnd_count):
    vmem = pl.BlockSpec(memory_space=pltpu.VMEM)
    smem = pl.BlockSpec(memory_space=pltpu.SMEM)
    dma = pltpu.SemaphoreType.DMA
    wide, slots = nodes.shape[1], bnd_index.shape[2]
    return pl.pallas_call(
        finish_kernel,
        out_shape=(
            jax.ShapeDtypeStruct((3, 2, wide), f32),
            jax.ShapeDtypeStruct((3, 2, 2 * slots), f32),
        ),
        in_specs=[vmem, vmem, vmem, smem],
        out_specs=(vmem, vmem),
        scratch_shapes=[
            pltpu.VMEM((4, 8, wide // 2), f32),
            pltpu.VMEM((24, 2 * slots), f32),
            pltpu.VMEM((8, 24, 2 * slots), f32),
            dma((3,)), dma((3,)), dma((8,)), dma((8,)),
        ],
        compiler_params=pltpu.CompilerParams(
            collective_id=1, has_side_effects=True, vmem_limit_bytes=32 * 1024 * 1024
        ),
        name="finish",
    )(disp, nodes, bnd_index, bnd_count)


def shards(nodes, surf_coords, surf_weights, tile_node, tile_surf, tile_count, bnd_index, bnd_count):
    n_table, s_table, w_table, codes, terms, early = gather(
        nodes,
        surf_coords.transpose(1, 0, 2),
        surf_weights.transpose(1, 0, 2),
        tile_node.transpose(0, 1, 3, 2),
        tile_surf.transpose(0, 1, 3, 2),
        tile_count,
    )
    disp = tiles(codes, n_table, s_table, w_table, terms, early)
    out, ghosts = finish(disp, nodes, bnd_index, bnd_count)
    return out.transpose(1, 0, 2), ghosts.transpose(1, 0, 2)


def solution(mesh):
    in_specs = (
        P(None, ("surf", "half")),
        P("inst", None, "surf"),
        P("inst", None, "surf"),
        P("surf", "half", None, None),
        P("surf", "half", None, None),
        P("surf", "half", None),
        P(("surf", "half"), None, None),
        P(("surf", "half"), None),
    )
    out_specs = (P("inst", None, ("surf", "half")), P("inst", None, ("surf", "half")))
    return jax.shard_map(shards, mesh=mesh, in_specs=in_specs, out_specs=out_specs, check_vma=False)
```

```python
import functools

import jax
import jax.numpy as jnp
from jax import lax
from jax.experimental import pallas as pl
from jax.experimental.pallas import tpu as pltpu
from jax.sharding import PartitionSpec as P

RADIUS = 0.4
HARMONIC = 0.8
CENTRE = 0.25
UNROLL = 48
TAIL = 16
EARLY = (32, 40, 48, 48)
PER_STEP = 24

f32 = jnp.float32
bf16 = jnp.bfloat16
MESH = pl.DeviceIdType.MESH
NN = (((1,), (0,)), ((), ()))
TN = (((0,), (0,)), ((), ()))


def split3(x):
    a = x.astype(bf16)
    rest = x - a.astype(f32)
    b = rest.astype(bf16)
    c = (rest - b.astype(f32)).astype(bf16)
    return a, b, c


def rows_of(shape):
    return lax.broadcasted_iota(jnp.int32, shape, 0)


def node_tables(nodes_ref, n_ref):
    row = rows_of((8, 128))
    blocks = nodes_ref.shape[1] // 128

    def one(b, _):
        x = (nodes_ref[:, pl.ds(pl.multiple_of(b * 128, 128), 128)] - CENTRE) * (1.0 / RADIUS)
        sq = x * x
        p = sq[0:1] + sq[1:2] + sq[2:3]
        four = jnp.concatenate([-2.0 * x, jnp.ones((1, 128), f32)], axis=0)
        eight = jnp.concatenate([four, four], axis=0)
        left, right = jnp.where(row < 4, eight, 0.0), jnp.where(row < 4, 0.0, eight)
        wide = jnp.concatenate([left, right], axis=1)
        b0, b1, b2 = split3(wide)
        p0, p1, p2 = split3(jnp.concatenate([p, p], axis=1))
        zero = jnp.zeros((13, 256), f32)
        tail = jnp.concatenate([p0.astype(f32), p1.astype(f32), p2.astype(f32), zero], axis=0).astype(bf16)
        n_ref[b, 0:16] = jnp.concatenate([b0, b0], axis=0)
        n_ref[b, 16:32] = jnp.concatenate([b1, b1], axis=0)
        n_ref[b, 32:48] = jnp.concatenate([b2, b0], axis=0)
        n_ref[b, 48:64] = tail
        return 0

    lax.fori_loop(0, blocks, one, 0)


def surface_tables(held, j, s_ref, w_ref):
    raw = jnp.concatenate([held[j, 0], held[j, 1]], axis=0)
    rest = held[j, 2]
    row = rows_of(raw.shape)
    c = (raw - CENTRE) * (1.0 / RADIUS)
    sq = c * c
    q = pltpu.roll(sq, 1, 0) + pltpu.roll(sq, 2, 0) + pltpu.roll(sq, 3, 0)
    a0, a1, a2 = split3(jnp.where(row % 4 == 3, q, c))
    first = jnp.concatenate([a0, a1], axis=0)
    second = jnp.concatenate([a0, a2], axis=0)
    w = jnp.concatenate([rest, rest[3:4], rest[0:3]], axis=0)
    w = jnp.where(row % 4 == 3, raw, w) * 4.0
    hi = w.astype(bf16)
    both = jnp.concatenate([hi, (w - hi.astype(f32)).astype(bf16)], axis=0)
    per = c.shape[1] // 128
    for b in range(per):
        at = slice(b * 128, b * 128 + 128)
        s_ref[j * per + b, 0:16] = first[:, at]
        s_ref[j * per + b, 16:32] = second[:, at]
        w_ref[j * per + b] = both[:, at]


def tile_sum(s, n, w):
    ones = jnp.ones((16, 128), bf16)
    left = jnp.concatenate([s[0:16], s[0:16], s[16:32], ones], axis=0)
    dist2 = lax.dot_general(left, n, TN, preferred_element_type=f32)
    dist = pl.reciprocal(lax.rsqrt(lax.clamp(0.0, dist2, 1.0)), approx=True)
    inner = 1.0 - dist
    inner2 = inner * inner
    phi = (inner2 * inner2) * (0.25 + dist)
    hi = phi.astype(bf16)
    lo = (phi - hi.astype(f32)).astype(bf16)
    return lax.dot_general(
        jnp.concatenate([w, w], axis=1), jnp.concatenate([hi, lo], axis=0), NN,
        preferred_element_type=f32,
    )


def compact(node_list, surf_list, counts, codes_ref, per, dummy, z, y_lo, ring):
    most, n = node_list.shape
    size = codes_ref.shape[1]
    lane = lax.broadcasted_iota(jnp.int32, (most, n), 1)
    code = node_list[...] * 512 + surf_list[...] + lane * per
    count = counts[...]
    wide = jnp.broadcast_to(count.astype(f32), (8, n)).astype(bf16)

    def apart(o):
        d = lax.rem(o // 4 + ring - z, ring)
        near = jnp.where(lax.rem(o, 4) // 2 == y_lo, 0, 1)
        return jnp.where(d == 0, near, jnp.where(d == 1, 2, jnp.where(d == ring - 1, 2, 3)))

    def key(o):
        return o + apart(o) * n

    earlier = key(rows_of((n, n))) < key(lax.broadcasted_iota(jnp.int32, (n, n), 1))
    earlier = earlier.astype(f32).astype(bf16)
    base = lax.dot_general(wide, earlier, NN, preferred_element_type=f32)[0:1].astype(jnp.int32)
    slot = rows_of((most, n))
    dest = jnp.where(slot < count, base + slot, -1)
    place = lax.broadcasted_iota(jnp.int32, (most, size), 1)
    found = jnp.zeros((most, size), jnp.int32)
    for o in range(n):
        found += jnp.where(dest[:, o:o + 1] == place, code[:, o:o + 1], 0)
    far = apart(lax.broadcasted_iota(jnp.int32, (1, n), 1))

    def within(d):
        held = jnp.where(far <= d, count, 0).astype(f32)
        return jnp.sum(held, axis=1, keepdims=True).astype(jnp.int32)

    total = within(3)
    line = lax.broadcasted_iota(jnp.int32, (1, size), 1)
    listed = jnp.sum(found, axis=0, keepdims=True) + jnp.where(line >= total, dummy, 0)
    for d in range(4):
        listed = jnp.where(line == size - 4 + d, within(d), listed)
    codes_ref[...] = listed


def gather_kernel(nodes_hbm, coords_hbm, weights_hbm, node_list_hbm, surf_list_hbm, counts_hbm,
                  n_ref, s_ref, w_ref, codes_ref, terms_ref, early_ref,
                  held, nodes_in, coords_in, weights_in, node_list, surf_list, counts, codes, local,
                  zs, zr, ys, yr, cs, cr):
    inst, surf, half = lax.axis_index("inst"), lax.axis_index("surf"), lax.axis_index("half")
    z, y_lo, core = surf // 4, (surf // 2) % 2, surf % 2
    ring = 8

    def at(zz, yy, cc):
        return (zz % ring) * 4 + yy * 2 + cc

    def along(d):
        return (inst, at(z + ring + d, y_lo, core), half)

    beside = (inst, at(z, 1 - y_lo, core), half)
    across = (inst, at(z, 1 - y_lo, core), 1 - half)
    twin = (inst, at(z, y_lo, 1 - core), half)

    barrier = pltpu.get_barrier_semaphore()
    for other in (along(1), along(-1), along(2), along(-2), beside, across, twin):
        pl.semaphore_signal(barrier, inc=1, device_id=other, device_id_type=MESH)
    pairs = (
        (coords_hbm, coords_in), (weights_hbm, weights_in), (nodes_hbm, nodes_in),
        (node_list_hbm.at[0, 0], node_list), (surf_list_hbm.at[0, 0], surf_list), (counts_hbm.at[0], counts),
    )
    loads = [pltpu.make_async_copy(src, dst, local.at[i]) for i, (src, dst) in enumerate(pairs)]
    for c in loads:
        c.start()
    per = coords_in.shape[2] // 128
    last = s_ref.shape[0] - 1
    s_ref[last] = jnp.zeros_like(s_ref[last])
    w_ref[last] = jnp.zeros_like(w_ref[last])
    mine = at(z, y_lo, core)
    loads[0].wait()
    loads[1].wait()
    c_in, w_in = coords_in, weights_in
    for i in range(2):
        held[mine, i] = jnp.concatenate([c_in[k, i:i + 1] for k in range(3)] + [w_in[0, i:i + 1]], axis=0)
    held[mine, 2] = jnp.concatenate([w_in[k, i:i + 1] for i in range(2) for k in (1, 2)], axis=0)

    mid = coords_in.shape[2] // 2
    low, high = pl.ds(0, mid), pl.ds(mid, mid)
    offsets = [0, -1, 1, -2, 2, -3, 3, 4]

    def copy(ref, send, recv, to):
        return pltpu.make_async_remote_copy(
            src_ref=ref, dst_ref=ref, send_sem=send, recv_sem=recv, device_id=to, device_id_type=MESH
        )

    def part(block, lanes=None):
        return held.at[block] if lanes is None else held.at[block, :, :, lanes]

    def own(d):
        return at(z + ring + d, y_lo, core)

    def other(d):
        return at(z + ring + d, 1 - y_lo, core)

    routes = {
        1: (1, 0, None), 2: (-1, 0, None), 3: (2, 0, None), 4: (-2, 0, None),
        5: (1, -2, None), 6: (-1, 2, None), 7: (2, -2, low), 0: (-2, 2, high),
    }

    def zcopy(r, arriving=False):
        step, origin, lanes = routes[r]
        block = own(origin - step) if arriving else own(origin)
        return copy(part(block, lanes), zs.at[r], zr.at[r], along(step))

    def ycopies(q, block):
        return (
            copy(part(block, low), ys.at[q], yr.at[q], beside),
            copy(part(block, high), ys.at[8 + q], yr.at[8 + q], across),
        )

    def ccopy(q, block):
        return copy(part(block), cs.at[q], cr.at[q], twin)

    sent = []

    def go(c):
        c.start()
        sent.append(c)

    def spread(q):
        for c in ycopies(q, own(offsets[q])):
            go(c)
        go(ccopy(q, own(offsets[q])))
        surface_tables(held, own(offsets[q]), s_ref, w_ref)

    def take_other(q):
        for c in ycopies(q, other(offsets[q])):
            c.wait_recv()
        go(ccopy(8 + q, other(offsets[q])))
        surface_tables(held, other(offsets[q]), s_ref, w_ref)

    pl.semaphore_wait(barrier, 7)
    for r in (1, 2, 3, 4):
        go(zcopy(r))
    spread(0)
    for c in loads[2:]:
        c.wait()
    node_tables(nodes_in, n_ref)
    compact(node_list, surf_list, counts, codes_ref, per, last, z, y_lo, ring)
    listing = pltpu.make_async_copy(codes_ref, codes, local.at[6])
    listing.start()
    size = codes_ref.shape[1]

    def batch(b, reach, start):
        limit = codes[0, size - 4 + reach]
        first = sum(EARLY[:b])
        for u in range(EARLY[b]):
            code = codes[0, jnp.clip(start + u, 0, size - 1)]
            code = jnp.where(start + u < limit, code, last)
            node = jnp.clip(lax.shift_right_logical(code, 9), 0, n_ref.shape[0] - 1)
            surf_block = jnp.clip(lax.bitwise_and(code, 511), 0, last)
            early_ref[0, first + u] = code
            terms_ref[first + u] = tile_sum(s_ref[surf_block], n_ref[node], w_ref[surf_block])
        return jnp.minimum(start + EARLY[b], limit)

    def take_twin(q):
        block = at(z + ring + offsets[q % 8], y_lo if q < 8 else 1 - y_lo, 1 - core)
        ccopy(q, block).wait_recv()
        surface_tables(held, block, s_ref, w_ref)

    zcopy(1, True).wait_recv()
    spread(1)
    zcopy(2, True).wait_recv()
    spread(2)
    take_other(0)
    take_twin(0)
    listing.wait()
    start = batch(0, 0, 0)
    zcopy(3, True).wait_recv()
    go(zcopy(5))
    go(zcopy(7))
    zcopy(4, True).wait_recv()
    go(zcopy(6))
    go(zcopy(0))
    spread(3)
    spread(4)
    take_twin(8)
    take_other(1)
    take_other(2)
    start = batch(1, 1, start)
    take_other(3)
    take_other(4)
    zcopy(5, True).wait_recv()
    spread(5)
    zcopy(6, True).wait_recv()
    spread(6)
    zcopy(7, True).wait_recv()
    zcopy(0, True).wait_recv()
    spread(7)
    for q in (1, 2, 9, 10):
        take_twin(q)
    start = batch(2, 2, start)
    for q in (5, 6, 7):
        take_other(q)
    for q in (3, 4, 11, 12):
        take_twin(q)
    start = batch(3, 2, start)
    early_ref[0, early_ref.shape[1] - 1] = start
    early_ref[0, sum(EARLY)] = last
    terms_ref[sum(EARLY)] = jnp.zeros((16, 256), f32)
    for q in (5, 6, 7, 13, 14, 15):
        take_twin(q)
    for c in sent:
        c.wait_send()


def gather(nodes, coords, weights, tile_node, tile_surf, tile_count):
    arrays = (nodes, coords, weights, tile_node, tile_surf, tile_count)
    n_surf = lax.axis_size("surf")
    points = coords.shape[2]
    blocks = n_surf * points // 128
    most, n = tile_node.shape[2:]
    size = most * n + 128
    vmem = pl.BlockSpec(memory_space=pltpu.VMEM)
    dma = pltpu.SemaphoreType.DMA
    return pl.pallas_call(
        gather_kernel,
        out_shape=(
            jax.ShapeDtypeStruct((nodes.shape[1] // 128, 64, 256), bf16),
            jax.ShapeDtypeStruct((blocks + 1, 32, 128), bf16),
            jax.ShapeDtypeStruct((blocks + 1, 16, 128), bf16),
            jax.ShapeDtypeStruct((1, size), jnp.int32),
            jax.ShapeDtypeStruct((sum(EARLY) + 1, 16, 256), f32),
            jax.ShapeDtypeStruct((1, 256), jnp.int32),
        ),
        in_specs=[pl.BlockSpec(memory_space=pltpu.HBM)] * 6,
        out_specs=(vmem,) * 5 + (pl.BlockSpec(memory_space=pltpu.SMEM),),
        scratch_shapes=[
            pltpu.VMEM((n_surf, 3, 4, points), f32),
            pltpu.VMEM(nodes.shape, f32),
            pltpu.VMEM(coords.shape, f32),
            pltpu.VMEM(weights.shape, f32),
            pltpu.VMEM((most, n), jnp.int32),
            pltpu.VMEM((most, n), jnp.int32),
            pltpu.VMEM((1, n), jnp.int32),
            pltpu.SMEM((1, size), jnp.int32),
            dma((7,)),
            dma((8,)), dma((8,)), dma((16,)), dma((16,)), dma((16,)), dma((16,)),
        ],
        compiler_params=pltpu.CompilerParams(
            collective_id=0, has_side_effects=True, vmem_limit_bytes=32 * 1024 * 1024
        ),
        name="gather",
    )(*(pltpu.with_memory_space_constraint(x, pltpu.HBM) for x in arrays))


def tiles_kernel(codes, early, n_ref, s_ref, w_ref, terms_ref, disp_ref, acc):
    total = codes[0, codes.shape[1] - 1]
    begin = early[0, early.shape[1] - 1]
    acc[...] = jnp.zeros_like(acc)
    given = terms_ref.shape[0] - 1

    def given_term(k):
        return lax.shift_right_logical(early[0, k], 9), terms_ref[k]

    def group(first, many, taken=None):
        found = []
        if taken is not None:
            found += [given_term(jnp.minimum(taken + j, given)) for j in range(PER_STEP)]
        for u in range(many):
            code = codes[0, first + u]
            node, surf = lax.shift_right_logical(code, 9), lax.bitwise_and(code, 511)
            found.append((node, tile_sum(s_ref[surf], n_ref[node], w_ref[surf])))
        for node, term in found:
            acc[node] += term
        return 0

    full = lax.div(total - begin, UNROLL)
    lax.fori_loop(0, full, lambda g, _: group(begin + g * UNROLL, UNROLL, g * PER_STEP), 0)

    def add_given(k, _):
        node, term = given_term(k)
        acc[node] += term
        return 0

    lax.fori_loop(jnp.minimum(full * PER_STEP, given), given, add_given, 0)
    rest = begin + full * UNROLL
    lax.fori_loop(0, lax.div(total - rest + (TAIL - 1), TAIL), lambda g, _: group(rest + g * TAIL, TAIL), 0)
    row = rows_of((8, 128))
    for b in range(acc.shape[0]):
        one = acc[b, 0:8] + acc[b, 8:16]
        a, c = one[:, 0:128], one[:, 128:256]
        first = jnp.where(row == 0, pltpu.roll(a, 5, 0), pltpu.roll(a, 1, 0))
        second = jnp.where(row == 5, pltpu.roll(c, 3, 0), pltpu.roll(c, 2, 0))
        second = jnp.where(row == 4, pltpu.roll(c, 5, 0), second)
        disp_ref[:, b * 128:b * 128 + 128] = jnp.where(row < 4, first, second)


def tiles(codes, n_table, s_table, w_table, terms, early):
    vmem = pl.BlockSpec(memory_space=pltpu.VMEM)
    smem = pl.BlockSpec(memory_space=pltpu.SMEM)
    node_blocks = n_table.shape[0]
    return pl.pallas_call(
        tiles_kernel,
        out_shape=jax.ShapeDtypeStruct((8, node_blocks * 128), f32),
        in_specs=[smem] * 2 + [vmem] * 4,
        out_specs=vmem,
        scratch_shapes=[pltpu.VMEM((node_blocks, 16, 256), f32)],
        compiler_params=pltpu.CompilerParams(vmem_limit_bytes=32 * 1024 * 1024),
        name="tiles",
    )(codes, early, n_table, s_table, w_table, terms)


def finish_kernel(disp_ref, nodes_ref, index_ref, count_ref, out_ref, ghost_ref,
                  part, outlist, inlist, xs, xr, gs, gr):
    inst, surf, half = lax.axis_index("inst"), lax.axis_index("surf"), lax.axis_index("half")
    n_inst, n_surf = 4, lax.axis_size("surf")
    peers = [((inst + d) % n_inst, surf, half) for d in range(1, n_inst)]
    ends = [(surf + n_surf - 1) % n_surf, (surf + 1) % n_surf]
    others = [((inst + d) % n_inst, ends[e], half) for e in range(2) for d in range(n_inst)]
    barrier = pltpu.get_barrier_semaphore()
    for to in peers + others:
        pl.semaphore_signal(barrier, inc=1, device_id=to, device_id_type=MESH)

    wide = disp_ref.shape[1]
    mid = wide // 2
    disp = disp_ref[...]
    both = disp + pltpu.roll(disp, 4, 0)
    part[0] = jnp.where(rows_of((8, mid)) < 4, both[:, :mid], both[:, mid:])
    pl.semaphore_wait(barrier, 3 * n_inst - 1)
    copies = [
        pltpu.make_async_remote_copy(
            src_ref=part.at[0], dst_ref=part.at[d], send_sem=xs.at[d - 1], recv_sem=xr.at[d - 1],
            device_id=peers[d - 1], device_id_type=MESH,
        )
        for d in range(1, n_inst)
    ]
    for c in copies:
        c.start()

    index = jnp.concatenate([index_ref[0, 0:1, :], index_ref[0, 1:2, :]], axis=1)
    slots = index.shape[1] // 2
    lane = lax.broadcasted_iota(jnp.int32, (8, 2 * slots), 1)
    live = lane < jnp.where(lane < slots, count_ref[0, 0], count_ref[0, 1] + slots)
    pick = (rows_of((128, 2 * slots)) == index % 128).astype(f32).astype(bf16)
    block = index // 128
    gap = jnp.zeros((1, wide), f32)
    nodes = nodes_ref[...]
    nodes8 = jnp.concatenate([nodes, gap, nodes, gap], axis=0)

    def picked(x):
        tall = jnp.concatenate([x[:, b * 128:b * 128 + 128] for b in range(wide // 128)], axis=0)
        lanes = sum(lax.dot_general(piece, pick, NN, preferred_element_type=f32) for piece in split3(tall))
        chosen = jnp.zeros((8, 2 * slots), f32)
        for b in range(wide // 128):
            chosen += jnp.where(block == b, lanes[b * 8:b * 8 + 8], 0.0)
        return chosen

    outlist[0:8] = picked(disp)
    outlist[8:16] = picked(nodes8)
    outlist[16:24] = jnp.where(live, 1.0, 0.0)
    lists = [
        pltpu.make_async_remote_copy(
            src_ref=outlist, dst_ref=inlist.at[i], send_sem=gs.at[i], recv_sem=gr.at[i],
            device_id=to, device_id_type=MESH,
        )
        for i, to in enumerate(others)
    ]
    for c in lists:
        c.start()

    for c in copies:
        c.wait_recv()
    total = (part[0] + part[1] + part[2] + part[3]) * (1.0 / (2 * n_inst))
    swapped = pltpu.roll(total, 4, 0)
    low = rows_of((8, mid)) < 4
    spectral = jnp.concatenate([jnp.where(low, total, swapped), jnp.where(low, swapped, total)], axis=1)
    deformed = nodes8 + spectral + HARMONIC * (disp - spectral)
    for k in range(3):
        out_ref[k] = jnp.concatenate([deformed[k:k + 1], deformed[4 + k:5 + k]], axis=0)

    for c in lists:
        c.wait_recv()

    def received(e):
        first = e * n_inst
        moved = inlist[first, 0:8]
        total = moved
        for d in range(1, n_inst):
            total += inlist[first + d, 0:8]
        mean = (total + pltpu.roll(total, 4, 0)) * (1.0 / (2 * n_inst))
        value = inlist[first, 8:16] + mean + HARMONIC * (moved - mean)
        return jnp.where(inlist[first, 16:24] > 0.5, value, 0.0)

    lower = jnp.where(surf > 0, received(1), 0.0)
    upper = jnp.where(surf < n_surf - 1, received(0), 0.0)
    shown = jnp.concatenate([lower[:, slots:], upper[:, :slots]], axis=1)
    for k in range(3):
        ghost_ref[k] = jnp.concatenate([shown[k:k + 1], shown[4 + k:5 + k]], axis=0)
    for c in copies + lists:
        c.wait_send()


def finish(disp, nodes, bnd_index, bnd_count):
    vmem = pl.BlockSpec(memory_space=pltpu.VMEM)
    smem = pl.BlockSpec(memory_space=pltpu.SMEM)
    dma = pltpu.SemaphoreType.DMA
    wide, slots = nodes.shape[1], bnd_index.shape[2]
    return pl.pallas_call(
        finish_kernel,
        out_shape=(
            jax.ShapeDtypeStruct((3, 2, wide), f32),
            jax.ShapeDtypeStruct((3, 2, 2 * slots), f32),
        ),
        in_specs=[vmem, vmem, vmem, smem],
        out_specs=(vmem, vmem),
        scratch_shapes=[
            pltpu.VMEM((4, 8, wide // 2), f32),
            pltpu.VMEM((24, 2 * slots), f32),
            pltpu.VMEM((8, 24, 2 * slots), f32),
            dma((3,)), dma((3,)), dma((8,)), dma((8,)),
        ],
        compiler_params=pltpu.CompilerParams(
            collective_id=1, has_side_effects=True, vmem_limit_bytes=32 * 1024 * 1024
        ),
        name="finish",
    )(disp, nodes, bnd_index, bnd_count)


def shards(nodes, surf_coords, surf_weights, tile_node, tile_surf, tile_count, bnd_index, bnd_count):
    n_table, s_table, w_table, codes, terms, early = gather(
        nodes,
        surf_coords.transpose(1, 0, 2),
        surf_weights.transpose(1, 0, 2),
        tile_node.transpose(0, 1, 3, 2),
        tile_surf.transpose(0, 1, 3, 2),
        tile_count,
    )
    disp = tiles(codes, n_table, s_table, w_table, terms, early)
    out, ghosts = finish(disp, nodes, bnd_index, bnd_count)
    return out.transpose(1, 0, 2), ghosts.transpose(1, 0, 2)


def solution(mesh):
    in_specs = (
        P(None, ("surf", "half")),
        P("inst", None, "surf"),
        P("inst", None, "surf"),
        P("surf", "half", None, None),
        P("surf", "half", None, None),
        P("surf", "half", None),
        P(("surf", "half"), None, None),
        P(("surf", "half"), None),
    )
    out_specs = (P("inst", None, ("surf", "half")), P("inst", None, ("surf", "half")))
    return jax.shard_map(shards, mesh=mesh, in_specs=in_specs, out_specs=out_specs, check_vma=False)
```

```python
import functools

import jax
import jax.numpy as jnp
from jax import lax
from jax.experimental import pallas as pl
from jax.experimental.pallas import tpu as pltpu
from jax.sharding import PartitionSpec as P

RADIUS = 0.4
HARMONIC = 0.8
CENTRE = 0.25
UNROLL = 48
TAIL = 16
EARLY = (32, 40, 48, 48)
PER_STEP = 24

f32 = jnp.float32
bf16 = jnp.bfloat16
MESH = pl.DeviceIdType.MESH
NN = (((1,), (0,)), ((), ()))
TN = (((0,), (0,)), ((), ()))


def split3(x):
    a = x.astype(bf16)
    rest = x - a.astype(f32)
    b = rest.astype(bf16)
    c = (rest - b.astype(f32)).astype(bf16)
    return a, b, c


def rows_of(shape):
    return lax.broadcasted_iota(jnp.int32, shape, 0)


def node_tables(nodes_ref, n_ref):
    row = rows_of((8, 128))
    blocks = nodes_ref.shape[1] // 128

    def one(b, _):
        x = (nodes_ref[:, pl.ds(pl.multiple_of(b * 128, 128), 128)] - CENTRE) * (1.0 / RADIUS)
        sq = x * x
        p = sq[0:1] + sq[1:2] + sq[2:3]
        four = jnp.concatenate([-2.0 * x, jnp.ones((1, 128), f32)], axis=0)
        eight = jnp.concatenate([four, four], axis=0)
        left, right = jnp.where(row < 4, eight, 0.0), jnp.where(row < 4, 0.0, eight)
        wide = jnp.concatenate([left, right], axis=1)
        b0, b1, b2 = split3(wide)
        p0, p1, p2 = split3(jnp.concatenate([p, p], axis=1))
        zero = jnp.zeros((13, 256), f32)
        tail = jnp.concatenate([p0.astype(f32), p1.astype(f32), p2.astype(f32), zero], axis=0).astype(bf16)
        n_ref[b, 0:16] = jnp.concatenate([b0, b0], axis=0)
        n_ref[b, 16:32] = jnp.concatenate([b1, b1], axis=0)
        n_ref[b, 32:48] = jnp.concatenate([b2, b0], axis=0)
        n_ref[b, 48:64] = tail
        return 0

    lax.fori_loop(0, blocks, one, 0)


def surface_tables(held, j, s_ref, w_ref):
    raw = jnp.concatenate([held[j, 0], held[j, 1]], axis=0)
    rest = held[j, 2]
    row = rows_of(raw.shape)
    c = (raw - CENTRE) * (1.0 / RADIUS)
    sq = c * c
    q = pltpu.roll(sq, 1, 0) + pltpu.roll(sq, 2, 0) + pltpu.roll(sq, 3, 0)
    a0, a1, a2 = split3(jnp.where(row % 4 == 3, q, c))
    first = jnp.concatenate([a0, a1], axis=0)
    second = jnp.concatenate([a0, a2], axis=0)
    w = jnp.concatenate([rest, rest[3:4], rest[0:3]], axis=0)
    w = jnp.where(row % 4 == 3, raw, w) * 4.0
    hi = w.astype(bf16)
    both = jnp.concatenate([hi, (w - hi.astype(f32)).astype(bf16)], axis=0)
    per = c.shape[1] // 128
    for b in range(per):
        at = slice(b * 128, b * 128 + 128)
        s_ref[j * per + b, 0:16] = first[:, at]
        s_ref[j * per + b, 16:32] = second[:, at]
        w_ref[j * per + b] = both[:, at]


def tile_sum(s, n, w):
    ones = jnp.ones((16, 128), bf16)
    left = jnp.concatenate([s[0:16], s[0:16], s[16:32], ones], axis=0)
    dist2 = lax.dot_general(left, n, TN, preferred_element_type=f32)
    dist = pl.reciprocal(lax.rsqrt(lax.clamp(0.0, dist2, 1.0)), approx=True)
    inner = 1.0 - dist
    inner2 = inner * inner
    phi = (inner2 * inner2) * (0.25 + dist)
    hi = phi.astype(bf16)
    lo = (phi - hi.astype(f32)).astype(bf16)
    return lax.dot_general(
        jnp.concatenate([w, w], axis=1), jnp.concatenate([hi, lo], axis=0), NN,
        preferred_element_type=f32,
    )


def compact(node_list, surf_list, counts, codes_ref, per, dummy, z, y_lo, ring):
    most, n = node_list.shape
    size = codes_ref.shape[1]
    lane = lax.broadcasted_iota(jnp.int32, (most, n), 1)
    code = node_list[...] * 512 + surf_list[...] + lane * per
    count = counts[...]
    wide = jnp.broadcast_to(count.astype(f32), (8, n)).astype(bf16)

    def apart(o):
        d = lax.rem(o // 4 + ring - z, ring)
        near = jnp.where(lax.rem(o, 4) // 2 == y_lo, 0, 1)
        return jnp.where(d == 0, near, jnp.where(d == 1, 2, jnp.where(d == ring - 1, 2, 3)))

    def key(o):
        return o + apart(o) * n

    earlier = key(rows_of((n, n))) < key(lax.broadcasted_iota(jnp.int32, (n, n), 1))
    earlier = earlier.astype(f32).astype(bf16)
    base = lax.dot_general(wide, earlier, NN, preferred_element_type=f32)[0:1].astype(jnp.int32)
    slot = rows_of((most, n))
    dest = jnp.where(slot < count, base + slot, -1)
    place = lax.broadcasted_iota(jnp.int32, (most, size), 1)
    found = jnp.zeros((most, size), jnp.int32)
    for o in range(n):
        found += jnp.where(dest[:, o:o + 1] == place, code[:, o:o + 1], 0)
    far = apart(lax.broadcasted_iota(jnp.int32, (1, n), 1))

    def within(d):
        held = jnp.where(far <= d, count, 0).astype(f32)
        return jnp.sum(held, axis=1, keepdims=True).astype(jnp.int32)

    total = within(3)
    line = lax.broadcasted_iota(jnp.int32, (1, size), 1)
    listed = jnp.sum(found, axis=0, keepdims=True) + jnp.where(line >= total, dummy, 0)
    for d in range(4):
        listed = jnp.where(line == size - 4 + d, within(d), listed)
    codes_ref[...] = listed


def gather_kernel(nodes_hbm, coords_hbm, weights_hbm, node_list_hbm, surf_list_hbm, counts_hbm,
                  n_ref, s_ref, w_ref, codes_ref, terms_ref, early_ref,
                  held, nodes_in, coords_in, weights_in, node_list, surf_list, counts, codes, local,
                  zs, zr, ys, yr, cs, cr):
    inst, surf, half = lax.axis_index("inst"), lax.axis_index("surf"), lax.axis_index("half")
    z, y_lo, core = surf // 4, (surf // 2) % 2, surf % 2
    ring = 8

    def at(zz, yy, cc):
        return (zz % ring) * 4 + yy * 2 + cc

    def along(d):
        return (inst, at(z + ring + d, y_lo, core), half)

    beside = (inst, at(z, 1 - y_lo, core), half)
    across = (inst, at(z, 1 - y_lo, core), 1 - half)
    twin = (inst, at(z, y_lo, 1 - core), half)

    barrier = pltpu.get_barrier_semaphore()
    for other in (along(1), along(-1), along(2), along(-2), beside, across, twin):
        pl.semaphore_signal(barrier, inc=1, device_id=other, device_id_type=MESH)
    pairs = (
        (coords_hbm, coords_in), (weights_hbm, weights_in), (nodes_hbm, nodes_in),
        (node_list_hbm.at[0, 0], node_list), (surf_list_hbm.at[0, 0], surf_list), (counts_hbm.at[0], counts),
    )
    loads = [pltpu.make_async_copy(src, dst, local.at[i]) for i, (src, dst) in enumerate(pairs)]
    for c in loads:
        c.start()
    per = coords_in.shape[2] // 128
    last = s_ref.shape[0] - 1
    s_ref[last] = jnp.zeros_like(s_ref[last])
    w_ref[last] = jnp.zeros_like(w_ref[last])
    mine = at(z, y_lo, core)
    loads[0].wait()
    loads[1].wait()
    c_in, w_in = coords_in, weights_in
    for i in range(2):
        held[mine, i] = jnp.concatenate([c_in[k, i:i + 1] for k in range(3)] + [w_in[0, i:i + 1]], axis=0)
    held[mine, 2] = jnp.concatenate([w_in[k, i:i + 1] for i in range(2) for k in (1, 2)], axis=0)

    mid = coords_in.shape[2] // 2
    low, high = pl.ds(0, mid), pl.ds(mid, mid)
    offsets = [0, -1, 1, -2, 2, -3, 3, 4]

    def copy(ref, send, recv, to):
        return pltpu.make_async_remote_copy(
            src_ref=ref, dst_ref=ref, send_sem=send, recv_sem=recv, device_id=to, device_id_type=MESH
        )

    def part(block, lanes=None):
        return held.at[block] if lanes is None else held.at[block, :, :, lanes]

    def own(d):
        return at(z + ring + d, y_lo, core)

    def other(d):
        return at(z + ring + d, 1 - y_lo, core)

    routes = {
        1: (1, 0, None), 2: (-1, 0, None), 3: (2, 0, None), 4: (-2, 0, None),
        5: (1, -2, None), 6: (-1, 2, None), 7: (2, -2, low), 0: (-2, 2, high),
    }

    def zcopy(r, arriving=False):
        step, origin, lanes = routes[r]
        block = own(origin - step) if arriving else own(origin)
        return copy(part(block, lanes), zs.at[r], zr.at[r], along(step))

    def ycopies(q, block):
        return (
            copy(part(block, low), ys.at[q], yr.at[q], beside),
            copy(part(block, high), ys.at[8 + q], yr.at[8 + q], across),
        )

    def ccopy(q, block):
        return copy(part(block), cs.at[q], cr.at[q], twin)

    sent = []

    def go(c):
        c.start()
        sent.append(c)

    def spread(q):
        for c in ycopies(q, own(offsets[q])):
            go(c)
        go(ccopy(q, own(offsets[q])))
        surface_tables(held, own(offsets[q]), s_ref, w_ref)

    def take_other(q):
        for c in ycopies(q, other(offsets[q])):
            c.wait_recv()
        go(ccopy(8 + q, other(offsets[q])))
        surface_tables(held, other(offsets[q]), s_ref, w_ref)

    pl.semaphore_wait(barrier, 7)
    for r in (1, 2, 3, 4):
        go(zcopy(r))
    spread(0)
    for c in loads[2:]:
        c.wait()
    node_tables(nodes_in, n_ref)
    compact(node_list, surf_list, counts, codes_ref, per, last, z, y_lo, ring)
    listing = pltpu.make_async_copy(codes_ref, codes, local.at[6])
    listing.start()
    size = codes_ref.shape[1]

    def batch(b, reach, start):
        limit = codes[0, size - 4 + reach]
        first = sum(EARLY[:b])
        for u in range(EARLY[b]):
            code = codes[0, jnp.clip(start + u, 0, size - 1)]
            code = jnp.where(start + u < limit, code, last)
            node = jnp.clip(lax.shift_right_logical(code, 9), 0, n_ref.shape[0] - 1)
            surf_block = jnp.clip(lax.bitwise_and(code, 511), 0, last)
            early_ref[0, first + u] = code
            terms_ref[first + u] = tile_sum(s_ref[surf_block], n_ref[node], w_ref[surf_block])
        return jnp.minimum(start + EARLY[b], limit)

    def take_twin(q):
        block = at(z + ring + offsets[q % 8], y_lo if q < 8 else 1 - y_lo, 1 - core)
        ccopy(q, block).wait_recv()
        surface_tables(held, block, s_ref, w_ref)

    zcopy(1, True).wait_recv()
    spread(1)
    zcopy(2, True).wait_recv()
    spread(2)
    take_other(0)
    take_twin(0)
    listing.wait()
    start = batch(0, 0, 0)
    zcopy(3, True).wait_recv()
    go(zcopy(5))
    go(zcopy(7))
    zcopy(4, True).wait_recv()
    go(zcopy(6))
    go(zcopy(0))
    spread(3)
    spread(4)
    take_twin(8)
    take_other(1)
    take_other(2)
    start = batch(1, 1, start)
    take_other(3)
    take_other(4)
    zcopy(5, True).wait_recv()
    spread(5)
    zcopy(6, True).wait_recv()
    spread(6)
    zcopy(7, True).wait_recv()
    zcopy(0, True).wait_recv()
    spread(7)
    for q in (1, 2, 9, 10):
        take_twin(q)
    start = batch(2, 2, start)
    for q in (5, 6, 7):
        take_other(q)
    for q in (3, 4, 11, 12):
        take_twin(q)
    start = batch(3, 2, start)
    early_ref[0, early_ref.shape[1] - 1] = start
    early_ref[0, sum(EARLY)] = last
    terms_ref[sum(EARLY)] = jnp.zeros((16, 256), f32)
    for q in (5, 6, 7, 13, 14, 15):
        take_twin(q)
    for c in sent:
        c.wait_send()


def gather(nodes, coords, weights, tile_node, tile_surf, tile_count):
    arrays = (nodes, coords, weights, tile_node, tile_surf, tile_count)
    n_surf = lax.axis_size("surf")
    points = coords.shape[2]
    blocks = n_surf * points // 128
    most, n = tile_node.shape[2:]
    size = most * n + 128
    vmem = pl.BlockSpec(memory_space=pltpu.VMEM)
    dma = pltpu.SemaphoreType.DMA
    return pl.pallas_call(
        gather_kernel,
        out_shape=(
            jax.ShapeDtypeStruct((nodes.shape[1] // 128, 64, 256), bf16),
            jax.ShapeDtypeStruct((blocks + 1, 32, 128), bf16),
            jax.ShapeDtypeStruct((blocks + 1, 16, 128), bf16),
            jax.ShapeDtypeStruct((1, size), jnp.int32),
            jax.ShapeDtypeStruct((sum(EARLY) + 1, 16, 256), f32),
            jax.ShapeDtypeStruct((1, 256), jnp.int32),
        ),
        in_specs=[pl.BlockSpec(memory_space=pltpu.HBM)] * 6,
        out_specs=(vmem,) * 5 + (pl.BlockSpec(memory_space=pltpu.SMEM),),
        scratch_shapes=[
            pltpu.VMEM((n_surf, 3, 4, points), f32),
            pltpu.VMEM(nodes.shape, f32),
            pltpu.VMEM(coords.shape, f32),
            pltpu.VMEM(weights.shape, f32),
            pltpu.VMEM((most, n), jnp.int32),
            pltpu.VMEM((most, n), jnp.int32),
            pltpu.VMEM((1, n), jnp.int32),
            pltpu.SMEM((1, size), jnp.int32),
            dma((7,)),
            dma((8,)), dma((8,)), dma((16,)), dma((16,)), dma((16,)), dma((16,)),
        ],
        compiler_params=pltpu.CompilerParams(
            collective_id=0, has_side_effects=True, vmem_limit_bytes=32 * 1024 * 1024
        ),
        name="gather",
    )(*(pltpu.with_memory_space_constraint(x, pltpu.HBM) for x in arrays))


def tiles_kernel(codes, early, n_ref, s_ref, w_ref, terms_ref, disp_ref, acc):
    total = codes[0, codes.shape[1] - 1]
    begin = early[0, early.shape[1] - 1]
    acc[...] = jnp.zeros_like(acc)
    given = terms_ref.shape[0] - 1

    def given_term(k):
        return lax.shift_right_logical(early[0, k], 9), terms_ref[k]

    def group(first, many, taken=None):
        found = []
        if taken is not None:
            found += [given_term(jnp.minimum(taken + j, given)) for j in range(PER_STEP)]
        for u in range(many):
            code = codes[0, first + u]
            node, surf = lax.shift_right_logical(code, 9), lax.bitwise_and(code, 511)
            found.append((node, tile_sum(s_ref[surf], n_ref[node], w_ref[surf])))
        for node, term in found:
            acc[node] += term
        return 0

    full = lax.div(total - begin, UNROLL)
    lax.fori_loop(0, full, lambda g, _: group(begin + g * UNROLL, UNROLL, g * PER_STEP), 0)

    def add_given(k, _):
        node, term = given_term(k)
        acc[node] += term
        return 0

    lax.fori_loop(jnp.minimum(full * PER_STEP, given), given, add_given, 0)
    rest = begin + full * UNROLL
    lax.fori_loop(0, lax.div(total - rest + (TAIL - 1), TAIL), lambda g, _: group(rest + g * TAIL, TAIL), 0)
    row = rows_of((8, 128))
    for b in range(acc.shape[0]):
        one = acc[b, 0:8] + acc[b, 8:16]
        a, c = one[:, 0:128], one[:, 128:256]
        first = jnp.where(row == 0, pltpu.roll(a, 5, 0), pltpu.roll(a, 1, 0))
        second = jnp.where(row == 5, pltpu.roll(c, 3, 0), pltpu.roll(c, 2, 0))
        second = jnp.where(row == 4, pltpu.roll(c, 5, 0), second)
        disp_ref[:, b * 128:b * 128 + 128] = jnp.where(row < 4, first, second)


def tiles(codes, n_table, s_table, w_table, terms, early):
    vmem = pl.BlockSpec(memory_space=pltpu.VMEM)
    smem = pl.BlockSpec(memory_space=pltpu.SMEM)
    node_blocks = n_table.shape[0]
    return pl.pallas_call(
        tiles_kernel,
        out_shape=jax.ShapeDtypeStruct((8, node_blocks * 128), f32),
        in_specs=[smem] * 2 + [vmem] * 4,
        out_specs=vmem,
        scratch_shapes=[pltpu.VMEM((node_blocks, 16, 256), f32)],
        compiler_params=pltpu.CompilerParams(vmem_limit_bytes=32 * 1024 * 1024),
        name="tiles",
    )(codes, early, n_table, s_table, w_table, terms)


def finish_kernel(disp_ref, nodes_ref, index_ref, count_ref, out_ref, ghost_ref,
                  part, outlist, inlist, xs, xr, gs, gr):
    inst, surf, half = lax.axis_index("inst"), lax.axis_index("surf"), lax.axis_index("half")
    n_inst, n_surf = 4, lax.axis_size("surf")
    peers = [((inst + d) % n_inst, surf, half) for d in range(1, n_inst)]
    ends = [(surf + n_surf - 1) % n_surf, (surf + 1) % n_surf]
    others = [((inst + d) % n_inst, ends[e], half) for e in range(2) for d in range(n_inst)]
    barrier = pltpu.get_barrier_semaphore()
    for to in peers + others:
        pl.semaphore_signal(barrier, inc=1, device_id=to, device_id_type=MESH)

    wide = disp_ref.shape[1]
    unit = wide // 8
    body = 3 * unit
    disp = disp_ref[...]
    both = disp + pltpu.roll(disp, 4, 0)
    row = rows_of((8, body))
    third = jnp.concatenate([pltpu.roll(both[:, 6 * unit:], 3, 0), pltpu.roll(both[:, 6 * unit:7 * unit], 2, 0)], axis=1)
    seventh = jnp.concatenate([pltpu.roll(both[:, 7 * unit:], 2, 0), pltpu.roll(both[:, 6 * unit:], 1, 0)], axis=1)
    packed = jnp.where(row < 4, both[:, :body], both[:, body:2 * body])
    part[0] = jnp.where(row == 3, third, jnp.where(row == 7, seventh, packed))
    pl.semaphore_wait(barrier, 3 * n_inst - 1)
    copies = [
        pltpu.make_async_remote_copy(
            src_ref=part.at[0], dst_ref=part.at[d], send_sem=xs.at[d - 1], recv_sem=xr.at[d - 1],
            device_id=peers[d - 1], device_id_type=MESH,
        )
        for d in range(1, n_inst)
    ]
    for c in copies:
        c.start()

    index = jnp.concatenate([index_ref[0, 0:1, :], index_ref[0, 1:2, :]], axis=1)
    slots = index.shape[1] // 2
    lane = lax.broadcasted_iota(jnp.int32, (8, 2 * slots), 1)
    live = lane < jnp.where(lane < slots, count_ref[0, 0], count_ref[0, 1] + slots)
    pick = (rows_of((128, 2 * slots)) == index % 128).astype(f32).astype(bf16)
    block = index // 128
    gap = jnp.zeros((1, wide), f32)
    nodes = nodes_ref[...]
    nodes8 = jnp.concatenate([nodes, gap, nodes, gap], axis=0)

    def picked(x):
        tall = jnp.concatenate([x[:, b * 128:b * 128 + 128] for b in range(wide // 128)], axis=0)
        lanes = sum(lax.dot_general(piece, pick, NN, preferred_element_type=f32) for piece in split3(tall))
        chosen = jnp.zeros((8, 2 * slots), f32)
        for b in range(wide // 128):
            chosen += jnp.where(block == b, lanes[b * 8:b * 8 + 8], 0.0)
        return chosen

    outlist[0:8] = picked(disp)
    outlist[8:16] = picked(nodes8)
    outlist[16:24] = jnp.where(live, 1.0, 0.0)
    lists = [
        pltpu.make_async_remote_copy(
            src_ref=outlist, dst_ref=inlist.at[i], send_sem=gs.at[i], recv_sem=gr.at[i],
            device_id=to, device_id_type=MESH,
        )
        for i, to in enumerate(others)
    ]
    for c in lists:
        c.start()

    for c in copies:
        c.wait_recv()
    total = (part[0] + part[1] + part[2] + part[3]) * (1.0 / (2 * n_inst))
    swapped = pltpu.roll(total, 4, 0)
    low = row < 4
    comp0 = pltpu.roll(total[:, :2 * unit], 5, 0)
    comp1 = jnp.concatenate([pltpu.roll(total[:, 2 * unit:], 6, 0), pltpu.roll(total[:, :unit], 2, 0)], axis=1)
    comp2 = pltpu.roll(total[:, unit:], 3, 0)
    tail_row = rows_of((8, 2 * unit))
    tail = jnp.where(tail_row == 0, comp0, jnp.where(tail_row == 1, comp1, comp2))
    tail = jnp.where(tail_row < 4, tail, pltpu.roll(tail, 4, 0))
    spectral = jnp.concatenate([jnp.where(low, total, swapped), jnp.where(low, swapped, total), tail], axis=1)
    deformed = nodes8 + spectral + HARMONIC * (disp - spectral)
    for k in range(3):
        out_ref[k] = jnp.concatenate([deformed[k:k + 1], deformed[4 + k:5 + k]], axis=0)

    for c in lists:
        c.wait_recv()

    def received(e):
        first = e * n_inst
        moved = inlist[first, 0:8]
        total = moved
        for d in range(1, n_inst):
            total += inlist[first + d, 0:8]
        mean = (total + pltpu.roll(total, 4, 0)) * (1.0 / (2 * n_inst))
        value = inlist[first, 8:16] + mean + HARMONIC * (moved - mean)
        return jnp.where(inlist[first, 16:24] > 0.5, value, 0.0)

    lower = jnp.where(surf > 0, received(1), 0.0)
    upper = jnp.where(surf < n_surf - 1, received(0), 0.0)
    shown = jnp.concatenate([lower[:, slots:], upper[:, :slots]], axis=1)
    for k in range(3):
        ghost_ref[k] = jnp.concatenate([shown[k:k + 1], shown[4 + k:5 + k]], axis=0)
    for c in copies + lists:
        c.wait_send()


def finish(disp, nodes, bnd_index, bnd_count):
    vmem = pl.BlockSpec(memory_space=pltpu.VMEM)
    smem = pl.BlockSpec(memory_space=pltpu.SMEM)
    dma = pltpu.SemaphoreType.DMA
    wide, slots = nodes.shape[1], bnd_index.shape[2]
    return pl.pallas_call(
        finish_kernel,
        out_shape=(
            jax.ShapeDtypeStruct((3, 2, wide), f32),
            jax.ShapeDtypeStruct((3, 2, 2 * slots), f32),
        ),
        in_specs=[vmem, vmem, vmem, smem],
        out_specs=(vmem, vmem),
        scratch_shapes=[
            pltpu.VMEM((4, 8, 3 * wide // 8), f32),
            pltpu.VMEM((24, 2 * slots), f32),
            pltpu.VMEM((8, 24, 2 * slots), f32),
            dma((3,)), dma((3,)), dma((8,)), dma((8,)),
        ],
        compiler_params=pltpu.CompilerParams(
            collective_id=1, has_side_effects=True, vmem_limit_bytes=32 * 1024 * 1024
        ),
        name="finish",
    )(disp, nodes, bnd_index, bnd_count)


def shards(nodes, surf_coords, surf_weights, tile_node, tile_surf, tile_count, bnd_index, bnd_count):
    n_table, s_table, w_table, codes, terms, early = gather(
        nodes,
        surf_coords.transpose(1, 0, 2),
        surf_weights.transpose(1, 0, 2),
        tile_node.transpose(0, 1, 3, 2),
        tile_surf.transpose(0, 1, 3, 2),
        tile_count,
    )
    disp = tiles(codes, n_table, s_table, w_table, terms, early)
    out, ghosts = finish(disp, nodes, bnd_index, bnd_count)
    return out.transpose(1, 0, 2), ghosts.transpose(1, 0, 2)


def solution(mesh):
    in_specs = (
        P(None, ("surf", "half")),
        P("inst", None, "surf"),
        P("inst", None, "surf"),
        P("surf", "half", None, None),
        P("surf", "half", None, None),
        P("surf", "half", None),
        P(("surf", "half"), None, None),
        P(("surf", "half"), None),
    )
    out_specs = (P("inst", None, ("surf", "half")), P("inst", None, ("surf", "half")))
    return jax.shard_map(shards, mesh=mesh, in_specs=in_specs, out_specs=out_specs, check_vma=False)
```

```python
import functools

import jax
import jax.numpy as jnp
from jax import lax
from jax.experimental import pallas as pl
from jax.experimental.pallas import tpu as pltpu
from jax.sharding import PartitionSpec as P

RADIUS = 0.4
HARMONIC = 0.8
CENTRE = 0.25
UNROLL = 48
TAIL = 16
EARLY = (32, 40, 48, 48)
PER_STEP = 24

f32 = jnp.float32
bf16 = jnp.bfloat16
MESH = pl.DeviceIdType.MESH
NN = (((1,), (0,)), ((), ()))
TN = (((0,), (0,)), ((), ()))


def split3(x):
    a = x.astype(bf16)
    rest = x - a.astype(f32)
    b = rest.astype(bf16)
    c = (rest - b.astype(f32)).astype(bf16)
    return a, b, c


def rows_of(shape):
    return lax.broadcasted_iota(jnp.int32, shape, 0)


def node_tables(nodes_ref, n_ref):
    row = rows_of((8, 128))
    blocks = nodes_ref.shape[1] // 128

    def one(b, _):
        x = (nodes_ref[:, pl.ds(pl.multiple_of(b * 128, 128), 128)] - CENTRE) * (1.0 / RADIUS)
        sq = x * x
        p = sq[0:1] + sq[1:2] + sq[2:3]
        four = jnp.concatenate([-2.0 * x, jnp.ones((1, 128), f32)], axis=0)
        eight = jnp.concatenate([four, four], axis=0)
        left, right = jnp.where(row < 4, eight, 0.0), jnp.where(row < 4, 0.0, eight)
        wide = jnp.concatenate([left, right], axis=1)
        b0, b1, b2 = split3(wide)
        p0, p1, p2 = split3(jnp.concatenate([p, p], axis=1))
        zero = jnp.zeros((13, 256), f32)
        tail = jnp.concatenate([p0.astype(f32), p1.astype(f32), p2.astype(f32), zero], axis=0).astype(bf16)
        n_ref[b, 0:16] = jnp.concatenate([b0, b0], axis=0)
        n_ref[b, 16:32] = jnp.concatenate([b1, b1], axis=0)
        n_ref[b, 32:48] = jnp.concatenate([b2, b0], axis=0)
        n_ref[b, 48:64] = tail
        return 0

    lax.fori_loop(0, blocks, one, 0)


def surface_tables(held, j, s_ref, w_ref):
    raw = jnp.concatenate([held[j, 0], held[j, 1]], axis=0)
    rest = held[j, 2]
    row = rows_of(raw.shape)
    c = (raw - CENTRE) * (1.0 / RADIUS)
    sq = c * c
    q = pltpu.roll(sq, 1, 0) + pltpu.roll(sq, 2, 0) + pltpu.roll(sq, 3, 0)
    a0, a1, a2 = split3(jnp.where(row % 4 == 3, q, c))
    first = jnp.concatenate([a0, a1], axis=0)
    second = jnp.concatenate([a0, a2], axis=0)
    w = jnp.concatenate([rest, rest[3:4], rest[0:3]], axis=0)
    w = jnp.where(row % 4 == 3, raw, w) * 4.0
    hi = w.astype(bf16)
    both = jnp.concatenate([hi, (w - hi.astype(f32)).astype(bf16)], axis=0)
    per = c.shape[1] // 128
    for b in range(per):
        at = slice(b * 128, b * 128 + 128)
        s_ref[j * per + b, 0:16] = first[:, at]
        s_ref[j * per + b, 16:32] = second[:, at]
        w_ref[j * per + b] = both[:, at]


def tile_sum(s, n, w):
    ones = jnp.ones((16, 128), bf16)
    left = jnp.concatenate([s[0:16], s[0:16], s[16:32], ones], axis=0)
    dist2 = lax.dot_general(left, n, TN, preferred_element_type=f32)
    dist = pl.reciprocal(lax.rsqrt(lax.clamp(0.0, dist2, 1.0)), approx=True)
    inner = 1.0 - dist
    inner2 = inner * inner
    phi = (inner2 * inner2) * (0.25 + dist)
    hi = phi.astype(bf16)
    lo = (phi - hi.astype(f32)).astype(bf16)
    return lax.dot_general(
        jnp.concatenate([w, w], axis=1), jnp.concatenate([hi, lo], axis=0), NN,
        preferred_element_type=f32,
    )


def compact(node_list, surf_list, counts, codes_ref, per, dummy, z, y_lo, ring):
    most, n = node_list.shape
    size = codes_ref.shape[1]
    lane = lax.broadcasted_iota(jnp.int32, (most, n), 1)
    code = node_list[...] * 512 + surf_list[...] + lane * per
    count = counts[...]
    wide = jnp.broadcast_to(count.astype(f32), (8, n)).astype(bf16)

    def apart(o):
        d = lax.rem(o // 4 + ring - z, ring)
        near = jnp.where(lax.rem(o, 4) // 2 == y_lo, 0, 1)
        return jnp.where(d == 0, near, jnp.where(d == 1, 2, jnp.where(d == ring - 1, 2, 3)))

    def key(o):
        return o + apart(o) * n

    earlier = key(rows_of((n, n))) < key(lax.broadcasted_iota(jnp.int32, (n, n), 1))
    earlier = earlier.astype(f32).astype(bf16)
    base = lax.dot_general(wide, earlier, NN, preferred_element_type=f32)[0:1].astype(jnp.int32)
    slot = rows_of((most, n))
    dest = jnp.where(slot < count, base + slot, -1)
    place = lax.broadcasted_iota(jnp.int32, (most, size), 1)
    found = jnp.zeros((most, size), jnp.int32)
    for o in range(n):
        found += jnp.where(dest[:, o:o + 1] == place, code[:, o:o + 1], 0)
    far = apart(lax.broadcasted_iota(jnp.int32, (1, n), 1))

    def within(d):
        held = jnp.where(far <= d, count, 0).astype(f32)
        return jnp.sum(held, axis=1, keepdims=True).astype(jnp.int32)

    total = within(3)
    line = lax.broadcasted_iota(jnp.int32, (1, size), 1)
    listed = jnp.sum(found, axis=0, keepdims=True) + jnp.where(line >= total, dummy, 0)
    for d in range(4):
        listed = jnp.where(line == size - 4 + d, within(d), listed)
    codes_ref[...] = listed


def gather_kernel(nodes_hbm, coords_hbm, weights_hbm, node_list_hbm, surf_list_hbm, counts_hbm,
                  n_ref, s_ref, w_ref, codes_ref, terms_ref, early_ref,
                  held, nodes_in, coords_in, weights_in, node_list, surf_list, counts, codes, local,
                  zs, zr, ys, yr, cs, cr):
    inst, surf, half = lax.axis_index("inst"), lax.axis_index("surf"), lax.axis_index("half")
    z, y_lo, core = surf // 4, (surf // 2) % 2, surf % 2
    ring = 8

    def at(zz, yy, cc):
        return (zz % ring) * 4 + yy * 2 + cc

    def along(d):
        return (inst, at(z + ring + d, y_lo, core), half)

    beside = (inst, at(z, 1 - y_lo, core), half)
    across = (inst, at(z, 1 - y_lo, core), 1 - half)
    twin = (inst, at(z, y_lo, 1 - core), half)

    barrier = pltpu.get_barrier_semaphore()
    for other in (along(1), along(-1), along(2), along(-2), beside, across, twin):
        pl.semaphore_signal(barrier, inc=1, device_id=other, device_id_type=MESH)
    pairs = (
        (coords_hbm, coords_in), (weights_hbm, weights_in), (nodes_hbm, nodes_in),
        (node_list_hbm.at[0, 0], node_list), (surf_list_hbm.at[0, 0], surf_list), (counts_hbm.at[0], counts),
    )
    loads = [pltpu.make_async_copy(src, dst, local.at[i]) for i, (src, dst) in enumerate(pairs)]
    for c in loads:
        c.start()
    per = coords_in.shape[2] // 128
    last = s_ref.shape[0] - 1
    s_ref[last] = jnp.zeros_like(s_ref[last])
    w_ref[last] = jnp.zeros_like(w_ref[last])
    mine = at(z, y_lo, core)
    loads[0].wait()
    loads[1].wait()
    c_in, w_in = coords_in, weights_in
    for i in range(2):
        held[mine, i] = jnp.concatenate([c_in[k, i:i + 1] for k in range(3)] + [w_in[0, i:i + 1]], axis=0)
    held[mine, 2] = jnp.concatenate([w_in[k, i:i + 1] for i in range(2) for k in (1, 2)], axis=0)

    mid = coords_in.shape[2] // 2
    low, high = pl.ds(0, mid), pl.ds(mid, mid)
    offsets = [0, -1, 1, -2, 2, -3, 3, 4]

    def copy(ref, send, recv, to):
        return pltpu.make_async_remote_copy(
            src_ref=ref, dst_ref=ref, send_sem=send, recv_sem=recv, device_id=to, device_id_type=MESH
        )

    def part(block, lanes=None):
        return held.at[block] if lanes is None else held.at[block, :, :, lanes]

    def own(d):
        return at(z + ring + d, y_lo, core)

    def other(d):
        return at(z + ring + d, 1 - y_lo, core)

    routes = {
        1: (1, 0, None), 2: (-1, 0, None), 3: (2, 0, None), 4: (-2, 0, None),
        5: (1, -2, None), 6: (-1, 2, None), 7: (2, -2, low), 0: (-2, 2, high),
    }

    def zcopy(r, arriving=False):
        step, origin, lanes = routes[r]
        block = own(origin - step) if arriving else own(origin)
        return copy(part(block, lanes), zs.at[r], zr.at[r], along(step))

    def ycopies(q, block):
        return (
            copy(part(block, low), ys.at[q], yr.at[q], beside),
            copy(part(block, high), ys.at[8 + q], yr.at[8 + q], across),
        )

    def ccopy(q, block):
        return copy(part(block), cs.at[q], cr.at[q], twin)

    sent = []

    def go(c):
        c.start()
        sent.append(c)

    def spread(q):
        for c in ycopies(q, own(offsets[q])):
            go(c)
        go(ccopy(q, own(offsets[q])))
        surface_tables(held, own(offsets[q]), s_ref, w_ref)

    def take_other(q):
        for c in ycopies(q, other(offsets[q])):
            c.wait_recv()
        go(ccopy(8 + q, other(offsets[q])))
        surface_tables(held, other(offsets[q]), s_ref, w_ref)

    pl.semaphore_wait(barrier, 7)
    for r in (3, 4, 1, 2):
        go(zcopy(r))
    spread(0)
    for c in loads[2:]:
        c.wait()
    node_tables(nodes_in, n_ref)
    compact(node_list, surf_list, counts, codes_ref, per, last, z, y_lo, ring)
    listing = pltpu.make_async_copy(codes_ref, codes, local.at[6])
    listing.start()
    size = codes_ref.shape[1]

    def batch(b, reach, start):
        limit = codes[0, size - 4 + reach]
        first = sum(EARLY[:b])
        for u in range(EARLY[b]):
            code = codes[0, jnp.clip(start + u, 0, size - 1)]
            code = jnp.where(start + u < limit, code, last)
            node = jnp.clip(lax.shift_right_logical(code, 9), 0, n_ref.shape[0] - 1)
            surf_block = jnp.clip(lax.bitwise_and(code, 511), 0, last)
            early_ref[0, first + u] = code
            terms_ref[first + u] = tile_sum(s_ref[surf_block], n_ref[node], w_ref[surf_block])
        return jnp.minimum(start + EARLY[b], limit)

    def take_twin(q):
        block = at(z + ring + offsets[q % 8], y_lo if q < 8 else 1 - y_lo, 1 - core)
        ccopy(q, block).wait_recv()
        surface_tables(held, block, s_ref, w_ref)

    zcopy(3, True).wait_recv()
    go(zcopy(5))
    go(zcopy(7))
    zcopy(4, True).wait_recv()
    go(zcopy(6))
    go(zcopy(0))
    zcopy(1, True).wait_recv()
    spread(1)
    zcopy(2, True).wait_recv()
    spread(2)
    spread(3)
    spread(4)
    take_other(0)
    take_twin(0)
    listing.wait()
    start = batch(0, 0, 0)
    take_twin(8)
    take_other(1)
    take_other(2)
    start = batch(1, 1, start)
    take_other(3)
    take_other(4)
    zcopy(5, True).wait_recv()
    spread(5)
    zcopy(6, True).wait_recv()
    spread(6)
    zcopy(7, True).wait_recv()
    zcopy(0, True).wait_recv()
    spread(7)
    for q in (1, 2, 9, 10):
        take_twin(q)
    start = batch(2, 2, start)
    for q in (5, 6, 7):
        take_other(q)
    for q in (3, 4, 11, 12):
        take_twin(q)
    start = batch(3, 2, start)
    early_ref[0, early_ref.shape[1] - 1] = start
    early_ref[0, sum(EARLY)] = last
    terms_ref[sum(EARLY)] = jnp.zeros((16, 256), f32)
    for q in (5, 6, 7, 13, 14, 15):
        take_twin(q)
    for c in sent:
        c.wait_send()


def gather(nodes, coords, weights, tile_node, tile_surf, tile_count):
    arrays = (nodes, coords, weights, tile_node, tile_surf, tile_count)
    n_surf = lax.axis_size("surf")
    points = coords.shape[2]
    blocks = n_surf * points // 128
    most, n = tile_node.shape[2:]
    size = most * n + 128
    vmem = pl.BlockSpec(memory_space=pltpu.VMEM)
    dma = pltpu.SemaphoreType.DMA
    return pl.pallas_call(
        gather_kernel,
        out_shape=(
            jax.ShapeDtypeStruct((nodes.shape[1] // 128, 64, 256), bf16),
            jax.ShapeDtypeStruct((blocks + 1, 32, 128), bf16),
            jax.ShapeDtypeStruct((blocks + 1, 16, 128), bf16),
            jax.ShapeDtypeStruct((1, size), jnp.int32),
            jax.ShapeDtypeStruct((sum(EARLY) + 1, 16, 256), f32),
            jax.ShapeDtypeStruct((1, 256), jnp.int32),
        ),
        in_specs=[pl.BlockSpec(memory_space=pltpu.HBM)] * 6,
        out_specs=(vmem,) * 5 + (pl.BlockSpec(memory_space=pltpu.SMEM),),
        scratch_shapes=[
            pltpu.VMEM((n_surf, 3, 4, points), f32),
            pltpu.VMEM(nodes.shape, f32),
            pltpu.VMEM(coords.shape, f32),
            pltpu.VMEM(weights.shape, f32),
            pltpu.VMEM((most, n), jnp.int32),
            pltpu.VMEM((most, n), jnp.int32),
            pltpu.VMEM((1, n), jnp.int32),
            pltpu.SMEM((1, size), jnp.int32),
            dma((7,)),
            dma((8,)), dma((8,)), dma((16,)), dma((16,)), dma((16,)), dma((16,)),
        ],
        compiler_params=pltpu.CompilerParams(
            collective_id=0, has_side_effects=True, vmem_limit_bytes=32 * 1024 * 1024
        ),
        name="gather",
    )(*(pltpu.with_memory_space_constraint(x, pltpu.HBM) for x in arrays))


def tiles_kernel(codes, early, n_ref, s_ref, w_ref, terms_ref, disp_ref, acc):
    total = codes[0, codes.shape[1] - 1]
    begin = early[0, early.shape[1] - 1]
    acc[...] = jnp.zeros_like(acc)
    given = terms_ref.shape[0] - 1

    def given_term(k):
        return lax.shift_right_logical(early[0, k], 9), terms_ref[k]

    def group(first, many, taken=None):
        found = []
        if taken is not None:
            found += [given_term(jnp.minimum(taken + j, given)) for j in range(PER_STEP)]
        for u in range(many):
            code = codes[0, first + u]
            node, surf = lax.shift_right_logical(code, 9), lax.bitwise_and(code, 511)
            found.append((node, tile_sum(s_ref[surf], n_ref[node], w_ref[surf])))
        for node, term in found:
            acc[node] += term
        return 0

    full = lax.div(total - begin, UNROLL)
    lax.fori_loop(0, full, lambda g, _: group(begin + g * UNROLL, UNROLL, g * PER_STEP), 0)

    def add_given(k, _):
        node, term = given_term(k)
        acc[node] += term
        return 0

    lax.fori_loop(jnp.minimum(full * PER_STEP, given), given, add_given, 0)
    rest = begin + full * UNROLL
    lax.fori_loop(0, lax.div(total - rest + (TAIL - 1), TAIL), lambda g, _: group(rest + g * TAIL, TAIL), 0)
    row = rows_of((8, 128))
    for b in range(acc.shape[0]):
        one = acc[b, 0:8] + acc[b, 8:16]
        a, c = one[:, 0:128], one[:, 128:256]
        first = jnp.where(row == 0, pltpu.roll(a, 5, 0), pltpu.roll(a, 1, 0))
        second = jnp.where(row == 5, pltpu.roll(c, 3, 0), pltpu.roll(c, 2, 0))
        second = jnp.where(row == 4, pltpu.roll(c, 5, 0), second)
        disp_ref[:, b * 128:b * 128 + 128] = jnp.where(row < 4, first, second)


def tiles(codes, n_table, s_table, w_table, terms, early):
    vmem = pl.BlockSpec(memory_space=pltpu.VMEM)
    smem = pl.BlockSpec(memory_space=pltpu.SMEM)
    node_blocks = n_table.shape[0]
    return pl.pallas_call(
        tiles_kernel,
        out_shape=jax.ShapeDtypeStruct((8, node_blocks * 128), f32),
        in_specs=[smem] * 2 + [vmem] * 4,
        out_specs=vmem,
        scratch_shapes=[pltpu.VMEM((node_blocks, 16, 256), f32)],
        compiler_params=pltpu.CompilerParams(vmem_limit_bytes=32 * 1024 * 1024),
        name="tiles",
    )(codes, early, n_table, s_table, w_table, terms)


def finish_kernel(disp_ref, nodes_ref, index_ref, count_ref, out_ref, ghost_ref,
                  part, outlist, inlist, xs, xr, gs, gr):
    inst, surf, half = lax.axis_index("inst"), lax.axis_index("surf"), lax.axis_index("half")
    n_inst, n_surf = 4, lax.axis_size("surf")
    peers = [((inst + d) % n_inst, surf, half) for d in range(1, n_inst)]
    ends = [(surf + n_surf - 1) % n_surf, (surf + 1) % n_surf]
    others = [((inst + d) % n_inst, ends[e], half) for e in range(2) for d in range(n_inst)]
    barrier = pltpu.get_barrier_semaphore()
    for to in peers + others:
        pl.semaphore_signal(barrier, inc=1, device_id=to, device_id_type=MESH)

    wide = disp_ref.shape[1]
    unit = wide // 8
    body = 3 * unit
    disp = disp_ref[...]
    both = disp + pltpu.roll(disp, 4, 0)
    row = rows_of((8, body))
    third = jnp.concatenate([pltpu.roll(both[:, 6 * unit:], 3, 0), pltpu.roll(both[:, 6 * unit:7 * unit], 2, 0)], axis=1)
    seventh = jnp.concatenate([pltpu.roll(both[:, 7 * unit:], 2, 0), pltpu.roll(both[:, 6 * unit:], 1, 0)], axis=1)
    packed = jnp.where(row < 4, both[:, :body], both[:, body:2 * body])
    part[0] = jnp.where(row == 3, third, jnp.where(row == 7, seventh, packed))
    pl.semaphore_wait(barrier, 3 * n_inst - 1)
    copies = [
        pltpu.make_async_remote_copy(
            src_ref=part.at[0], dst_ref=part.at[d], send_sem=xs.at[d - 1], recv_sem=xr.at[d - 1],
            device_id=peers[d - 1], device_id_type=MESH,
        )
        for d in range(1, n_inst)
    ]
    for c in copies:
        c.start()

    index = jnp.concatenate([index_ref[0, 0:1, :], index_ref[0, 1:2, :]], axis=1)
    slots = index.shape[1] // 2
    lane = lax.broadcasted_iota(jnp.int32, (8, 2 * slots), 1)
    live = lane < jnp.where(lane < slots, count_ref[0, 0], count_ref[0, 1] + slots)
    pick = (rows_of((128, 2 * slots)) == index % 128).astype(f32).astype(bf16)
    block = index // 128
    gap = jnp.zeros((1, wide), f32)
    nodes = nodes_ref[...]
    nodes8 = jnp.concatenate([nodes, gap, nodes, gap], axis=0)

    def picked(x):
        tall = jnp.concatenate([x[:, b * 128:b * 128 + 128] for b in range(wide // 128)], axis=0)
        lanes = sum(lax.dot_general(piece, pick, NN, preferred_element_type=f32) for piece in split3(tall))
        chosen = jnp.zeros((8, 2 * slots), f32)
        for b in range(wide // 128):
            chosen += jnp.where(block == b, lanes[b * 8:b * 8 + 8], 0.0)
        return chosen

    outlist[0:8] = picked(disp)
    outlist[8:16] = picked(nodes8)
    outlist[16:24] = jnp.where(live, 1.0, 0.0)
    lists = [
        pltpu.make_async_remote_copy(
            src_ref=outlist, dst_ref=inlist.at[i], send_sem=gs.at[i], recv_sem=gr.at[i],
            device_id=to, device_id_type=MESH,
        )
        for i, to in enumerate(others)
    ]
    for c in lists:
        c.start()

    for c in copies:
        c.wait_recv()
    total = (part[0] + part[1] + part[2] + part[3]) * (1.0 / (2 * n_inst))
    swapped = pltpu.roll(total, 4, 0)
    low = row < 4
    comp0 = pltpu.roll(total[:, :2 * unit], 5, 0)
    comp1 = jnp.concatenate([pltpu.roll(total[:, 2 * unit:], 6, 0), pltpu.roll(total[:, :unit], 2, 0)], axis=1)
    comp2 = pltpu.roll(total[:, unit:], 3, 0)
    tail_row = rows_of((8, 2 * unit))
    tail = jnp.where(tail_row == 0, comp0, jnp.where(tail_row == 1, comp1, comp2))
    tail = jnp.where(tail_row < 4, tail, pltpu.roll(tail, 4, 0))
    spectral = jnp.concatenate([jnp.where(low, total, swapped), jnp.where(low, swapped, total), tail], axis=1)
    deformed = nodes8 + spectral + HARMONIC * (disp - spectral)
    for k in range(3):
        out_ref[k] = jnp.concatenate([deformed[k:k + 1], deformed[4 + k:5 + k]], axis=0)

    for c in lists:
        c.wait_recv()

    def received(e):
        first = e * n_inst
        moved = inlist[first, 0:8]
        total = moved
        for d in range(1, n_inst):
            total += inlist[first + d, 0:8]
        mean = (total + pltpu.roll(total, 4, 0)) * (1.0 / (2 * n_inst))
        value = inlist[first, 8:16] + mean + HARMONIC * (moved - mean)
        return jnp.where(inlist[first, 16:24] > 0.5, value, 0.0)

    lower = jnp.where(surf > 0, received(1), 0.0)
    upper = jnp.where(surf < n_surf - 1, received(0), 0.0)
    shown = jnp.concatenate([lower[:, slots:], upper[:, :slots]], axis=1)
    for k in range(3):
        ghost_ref[k] = jnp.concatenate([shown[k:k + 1], shown[4 + k:5 + k]], axis=0)
    for c in copies + lists:
        c.wait_send()


def finish(disp, nodes, bnd_index, bnd_count):
    vmem = pl.BlockSpec(memory_space=pltpu.VMEM)
    smem = pl.BlockSpec(memory_space=pltpu.SMEM)
    dma = pltpu.SemaphoreType.DMA
    wide, slots = nodes.shape[1], bnd_index.shape[2]
    return pl.pallas_call(
        finish_kernel,
        out_shape=(
            jax.ShapeDtypeStruct((3, 2, wide), f32),
            jax.ShapeDtypeStruct((3, 2, 2 * slots), f32),
        ),
        in_specs=[vmem, vmem, vmem, smem],
        out_specs=(vmem, vmem),
        scratch_shapes=[
            pltpu.VMEM((4, 8, 3 * wide // 8), f32),
            pltpu.VMEM((24, 2 * slots), f32),
            pltpu.VMEM((8, 24, 2 * slots), f32),
            dma((3,)), dma((3,)), dma((8,)), dma((8,)),
        ],
        compiler_params=pltpu.CompilerParams(
            collective_id=1, has_side_effects=True, vmem_limit_bytes=32 * 1024 * 1024
        ),
        name="finish",
    )(disp, nodes, bnd_index, bnd_count)


def shards(nodes, surf_coords, surf_weights, tile_node, tile_surf, tile_count, bnd_index, bnd_count):
    n_table, s_table, w_table, codes, terms, early = gather(
        nodes,
        surf_coords.transpose(1, 0, 2),
        surf_weights.transpose(1, 0, 2),
        tile_node.transpose(0, 1, 3, 2),
        tile_surf.transpose(0, 1, 3, 2),
        tile_count,
    )
    disp = tiles(codes, n_table, s_table, w_table, terms, early)
    out, ghosts = finish(disp, nodes, bnd_index, bnd_count)
    return out.transpose(1, 0, 2), ghosts.transpose(1, 0, 2)


def solution(mesh):
    in_specs = (
        P(None, ("surf", "half")),
        P("inst", None, "surf"),
        P("inst", None, "surf"),
        P("surf", "half", None, None),
        P("surf", "half", None, None),
        P("surf", "half", None),
        P(("surf", "half"), None, None),
        P(("surf", "half"), None),
    )
    out_specs = (P("inst", None, ("surf", "half")), P("inst", None, ("surf", "half")))
    return jax.shard_map(shards, mesh=mesh, in_specs=in_specs, out_specs=out_specs, check_vma=False)
```
